128 devices in a mesh: row: 32 (over x, z, y_lo), col: 4 (over y_hi, core).
Axes of the slice: x: 4, y: 4 (y_hi: 2, y_lo: 2; y = y_hi * 2 + y_lo), z: 4, core: 2. Of those that a mesh axis runs over, the one named last changes fastest.
Arguments:
- contrib: float32 [2, 8192, 8192], P(None, 'row', 'col'), may hold values from -4 to 4
- target_rows: int32 [2, 8192], P(None, 'row'), may hold values from 0 to 8191, as said below
- diag_shift: float32 [2, 1, 32, 256], P(None, None, 'row'), may hold values from 300 to 600
- pattern: int32 [2, 32], replicated, may hold values 0 or 1
Outputs:
- factored: float32 [2, 1, 32, 256, 8, 4, 256], P(None, None, 'row', None, None, 'col')
The draws below stay inside these ranges and needn't reach their ends.
Inputs may be any that keep to these rules, and one draw needn't show every extreme that they name: `target_rows`: each entry is a row of its front. Call the grid row of a front row i the value (i // 256) modulo the size of the row axis. Of the 256 rows of one row-axis index (an aligned block of one front), at most 16 have targets on any one grid row; in each front one grid row receives exactly 16 from every index.
All inputs are finite; a program needn't handle non-finite values.
Results may differ from the reference program's by a relative error of at most 0.00005.
Values sent between devices are 32-bit elements; how exact they have to be, the bound alone decides.
No kernel may reach another device: no remote copies, remote signals or barrier semaphores. Data moves between devices by JAX's collectives and lax.ppermute only.
A program may use at most 256 MiB of HBM per device.

```python
import jax
import jax.numpy as jnp
from jax import lax

F = 8192
P_SIZE = 1024
BS = 256
SRC = 256
ROWS = 8192
NB = 32
LA = 1
LB = 8
MOSTR = 16
N_ROW = 32
N_COL = 4


def draw_contrib(key, part):
    key = jax.random.fold_in(key, 5)
    key_vals = jax.random.fold_in(key, 0)
    values = jax.random.truncated_normal(key_vals, -4.0, 4.0, (2, ROWS, F), jnp.float32)
    return values.astype(jnp.float32)


def draw_target_rows(key, part):
    key = jax.random.fold_in(key, 11)
    key_hot, key_perm, key_block, key_offset = jax.random.split(key, 4)
    hot_rows = jax.random.randint(key_hot, (2,), 0, N_ROW)
    slots = jnp.arange(SRC, dtype=jnp.int32)
    relative = jnp.where(slots < MOSTR, 0, 1 + (slots - MOSTR) % (N_ROW - 1)).astype(jnp.int32)
    perm_keys = jax.random.split(key_perm, 2 * N_ROW)
    orders = jax.vmap(lambda one_key: jax.random.permutation(one_key, SRC))(perm_keys).reshape(2, N_ROW, SRC)
    grid_rows = (hot_rows[:, None, None] + relative[orders]) % N_ROW
    block_pick = jax.random.randint(key_block, (2, N_ROW, SRC), 0, LA)
    offsets = jax.random.randint(key_offset, (2, N_ROW, SRC), 0, BS)
    rows_out = (block_pick * N_ROW + grid_rows) * BS + offsets
    return rows_out.reshape(2, N_ROW * SRC).astype(jnp.int32)


def touch_ends(entries, rng, least, largest):
    spot = [jax.random.randint(jax.random.fold_in(rng, axis), (), 0, length) for axis, length in enumerate(entries.shape)]
    main_axis = entries.shape.index(max(entries.shape))
    next_to = spot[:main_axis] + [(spot[main_axis] + 1) % entries.shape[main_axis]] + spot[main_axis + 1:]
    return entries.at[tuple(spot)].set(least).at[tuple(next_to)].set(largest)


def block_scale(rng, extent, pieces, least, largest):
    loudness = 1.0
    for axis_at, parts in pieces:
        heights = jax.random.uniform(jax.random.fold_in(jax.random.fold_in(rng, 6), axis_at), (parts,), jnp.float32, least / len(pieces), largest / len(pieces))
        loudness = loudness * jnp.repeat(jnp.exp(heights), extent[axis_at] // parts).reshape((-1,) + (1,) * (len(extent) - 1 - axis_at))
    return loudness


def setup_inputs(seed: int = 0) -> dict:
    arg_keys = jax.random.split(jax.random.key(seed), 5)
    contrib = draw_contrib(jax.random.fold_in(arg_keys[4], 71), 0)
    target_rows = draw_target_rows(jax.random.fold_in(arg_keys[4], 71), 0)
    diag_shift = jnp.clip(300.0 + 300.0 * jax.random.uniform(arg_keys[2], (2, LA, N_ROW, BS), jnp.float32) ** block_scale(arg_keys[2], (2, LA, N_ROW, BS), ((2, 32),), -0.2, 0.2), 300.0, 600.0)
    pattern = touch_ends((jax.random.randint(arg_keys[3], (2, NB), 0, 4) < 3).astype(jnp.int32), jax.random.fold_in(arg_keys[3], 1), 0, 1)
    return {"contrib": contrib, "target_rows": target_rows, "diag_shift": diag_shift, "pattern": pattern}


def one_front(contrib_rows, targets, shifts, keep_table):
    positions = jnp.arange(F, dtype=jnp.int32)
    assembled = jnp.zeros((F, F), jnp.float32).at[targets].add(contrib_rows)
    assembled = assembled.at[positions, positions].add(shifts)
    block_of = positions // BS
    keep_rows = jnp.where(block_of < P_SIZE // BS, 1.0, keep_table[block_of].astype(jnp.float32)).astype(jnp.float32)
    in_panel = positions < P_SIZE
    scaling = jnp.where(in_panel[None, :], keep_rows[:, None], 1.0) * jnp.where(in_panel[:, None], keep_rows[None, :], 1.0)
    masked = assembled * scaling.astype(jnp.float32)
    corner = masked[:P_SIZE, :P_SIZE]
    lower_factor = jnp.linalg.cholesky(0.5 * (corner + corner.T))
    left_factor = jax.scipy.linalg.solve_triangular(lower_factor, masked[P_SIZE:, :P_SIZE].T, lower=True).T
    upper_factor = jax.scipy.linalg.solve_triangular(lower_factor, masked[:P_SIZE, P_SIZE:], lower=True)
    schur = masked[P_SIZE:, P_SIZE:] - jnp.dot(left_factor, upper_factor, precision=lax.Precision.HIGHEST)
    top_part = jnp.concatenate([lower_factor, masked[:P_SIZE, P_SIZE:]], axis=1)
    bottom_part = jnp.concatenate([left_factor, schur], axis=1)
    result = jnp.concatenate([top_part, bottom_part], axis=0)
    return result.reshape(LA, N_ROW, BS, LB, N_COL, BS)

def reference(contrib, target_rows, diag_shift, pattern):
    shifts = diag_shift.reshape(2, F)
    fronts = [one_front(contrib[which], target_rows[which], shifts[which], pattern[which]) for which in range(2)]
    return jnp.stack(fronts, axis=0)
```

```python
import jax
import jax.numpy as jnp
from jax import lax
from jax.experimental import pallas as pl
from jax.experimental.pallas import tpu as pltpu
from jax.sharding import PartitionSpec as P

F = 8192
P_SIZE = 1024
BS = 256
HI = lax.Precision.HIGHEST
VM = pl.BlockSpec(memory_space=pltpu.VMEM)
SM = pl.BlockSpec(memory_space=pltpu.SMEM)
F32 = jnp.float32


def params():
    return pltpu.CompilerParams(vmem_limit_bytes=60 * 1024 * 1024)


def dot_nn(a, b):
    return lax.dot_general(a, b, (((1,), (0,)), ((), ())), precision=HI, preferred_element_type=F32)


def dot_nt(a, b):
    return lax.dot_general(a, b, (((1,), (1,)), ((), ())), precision=HI, preferred_element_type=F32)


def dot_tn(a, b):
    return lax.dot_general(a, b, (((0,), (0,)), ((), ())), precision=HI, preferred_element_type=F32)


def build_kernel(pos_ref, t_ref, x_ref, diag_ref, main_ref, panel_ref, marks_ref, buf, cnt):
    my_col = pos_ref[1]
    for f in range(2):
        for j in range(16):
            block, half = j // 2, j % 2
            place = (block % 4) * 4 + (block // 4) * 2 + half
            buf[pl.ds(f * 4096 + place, 256, stride=16), :] = x_ref[f, :, j * 128:(j + 1) * 128]

    def clear(i, _):
        cnt[i] = 0
        for k in range(16):
            marks_ref[i // 2, (i % 2) * 16 + k] = 256
        return 0

    lax.fori_loop(0, 64, clear, 0)
    for i in range(32):
        f = i // 16
        panel_ref[pl.ds(i * 72 + 64, 2), :] = diag_ref[f]
    for f in range(2):

        def place_row(i, _):
            target = t_ref[f, i]
            owner = target // 256
            slot = cnt[f * 32 + owner]
            cnt[f * 32 + owner] = slot + 1
            marks_ref[owner, f * 16 + slot] = target % 256
            source = (f * 256 + i) * 16

            @pl.when(owner >= 4)
            def _():
                for c in range(4):
                    dest = (((owner * 4 + c) * 2 + f) * 16 + slot) * 4
                    main_ref[pl.ds(dest, 4), :] = buf[pl.ds(source + c * 4, 4), :]

            @pl.when(owner < 4)
            def _():
                for c in range(4):
                    q = (c - my_col + 4) % 4
                    for u in range(2):
                        for h in range(2):
                            dest = f * 16 + u * 8 + q * 2 + h
                            panel_ref[pl.ds(dest * 72 + owner * 16 + slot, 1), :] = (
                                buf[pl.ds(source + c * 4 + u * 2 + h, 1), :]
                            )

            return 0

        lax.fori_loop(0, 256, place_row, 0)


def build(pos, targets, contrib, diag):
    return pl.pallas_call(
        build_kernel,
        out_shape=(
            jax.ShapeDtypeStruct((16384, 128), F32),
            jax.ShapeDtypeStruct((32 * 72, 128), F32),
            jax.ShapeDtypeStruct((32, 32), jnp.int32),
        ),
        in_specs=[SM, SM, VM, VM],
        out_specs=(VM, VM, SM),
        scratch_shapes=[pltpu.VMEM((8192, 128), F32), pltpu.SMEM((64,), jnp.int32)],
        compiler_params=params(),
    )(pos, targets, contrib, diag)


def eye128():
    return (
        lax.broadcasted_iota(jnp.int32, (128, 128), 0) == lax.broadcasted_iota(jnp.int32, (128, 128), 1)
    ).astype(F32)


def panel_kernel(pos_ref, marks_ref, pattern_ref, x_ref, out_ref, acc):
    my_row, my_col = pos_ref[0], pos_ref[1]
    f, u, q, h = my_row // 16, (my_row // 8) % 2, (my_row // 2) % 4, my_row % 2
    block = 8 * my_col + u * 4 + (q + my_col) % 4
    for n in range(4):
        acc[n] = jnp.zeros((1032, 128), F32)

    def source(s, _):
        def step(k, _):
            for n in range(4):
                mark = marks_ref[s, 32 + n * 16 + k]
                row = jnp.where(mark == 256, 1024, n * 256 + mark)
                acc[n, pl.ds(row, 1), :] += x_ref[pl.ds(s * 72 + n * 16 + k, 1), :]
            return 0

        return lax.fori_loop(0, 16, step, 0, unroll=4)

    lax.fori_loop(0, 32, source, 0)
    scale = jnp.where(block >= 4, pattern_ref[f, block], 1).astype(F32)
    for n in range(4):
        out_ref[pl.ds(n * 256, 256), :] = acc[n, n * 256:(n + 1) * 256, :] * scale

    @pl.when(block < 4)
    def _():
        start = pl.multiple_of(block * 256 + h * 128, 128)
        shift = x_ref[pl.ds(block * 72 + 64 + h, 1), :]
        out_ref[pl.ds(start, 128), :] += eye128() * shift


def panel_piece(pos, marks, pattern, received):
    return pl.pallas_call(
        panel_kernel,
        out_shape=jax.ShapeDtypeStruct((1024, 128), F32),
        in_specs=[SM, SM, SM, VM],
        out_specs=VM,
        scratch_shapes=[pltpu.VMEM((4, 1032, 128), F32)],
        compiler_params=params(),
    )(pos, marks, pattern, received)


SRCS = 8


def assemble_kernel(pos_ref, marks_ref, pattern_ref, diag_ref, x_ref, out_ref, left_ref, acc):
    step = pl.program_id(0)
    my_row, my_col = pos_ref[0], pos_ref[1]

    @pl.when(step == 0)
    def _():
        acc[...] = jnp.zeros_like(acc)

    def source(s, _):
        def slot(k, _):
            for f in range(2):
                mark = marks_ref[step * SRCS + s, f * 16 + k]

                @pl.when(mark < 256)
                def _():
                    for c in range(4):
                        piece = x_ref[pl.ds((((s * 4 + c) * 2 + f) * 16 + k) * 4, 4), :]
                        acc[f, pl.ds(mark * 16 + c * 4, 4), :] += piece

            return 0

        return lax.fori_loop(0, 16, slot, 0)

    lax.fori_loop(0, SRCS, source, 0)

    @pl.when(step == pl.num_programs(0) - 1)
    def _():
        for f in range(2):
            scale = jnp.where(my_row >= 4, pattern_ref[f, my_row], 1).astype(F32)

            @pl.when(my_row % 4 == my_col)
            def _():
                for h in range(2):
                    at = pl.ds(h * 2048 + (my_row // 4) * 2 + h, 128, stride=16)
                    acc[f, at, :] += eye128() * diag_ref[f, h:h + 1, :]

            for h in range(2):
                left_ref[f, :, h * 128:(h + 1) * 128] = acc[f, pl.ds(h, 256, stride=16), :] * scale
            out_ref[f] = acc[f]


def assemble(pos, marks, pattern, diag, received):
    chunk = SRCS * 512
    return pl.pallas_call(
        assemble_kernel,
        grid=(32 // SRCS,),
        out_shape=(
            jax.ShapeDtypeStruct((2, 4096, 128), F32),
            jax.ShapeDtypeStruct((2, 256, 256), F32),
        ),
        in_specs=[SM, SM, SM, VM, pl.BlockSpec((chunk, 128), lambda s: (s, 0))],
        out_specs=(
            pl.BlockSpec((2, 4096, 128), lambda s: (0, 0, 0)),
            pl.BlockSpec((2, 256, 256), lambda s: (0, 0, 0)),
        ),
        scratch_shapes=[pltpu.VMEM((2, 4096, 128), F32)],
        compiler_params=params(),
    )(pos, marks, pattern, diag, received)


def factor_kernel(pos_ref, c_ref, l_ref, x_ref, d_ref):
    my_row, my_col = pos_ref[0], pos_ref[1]
    lanes = lax.broadcasted_iota(jnp.int32, (8, 128), 1)
    subs = lax.broadcasted_iota(jnp.int32, (8, 128), 0)
    low = lax.broadcasted_iota(jnp.int32, (128, 128), 0) >= lax.broadcasted_iota(jnp.int32, (128, 128), 1)

    def corner(f, rows, block):
        other = jnp.bitwise_xor(block // 2, my_col)
        return c_ref[other % 2, other // 2, f, jnp.bitwise_xor(block % 2, my_row % 2), pl.ds(rows * 128, 128), :]

    def symmetrize(f, _):
        for i in range(8):
            for j in range(i + 1):
                l_ref[f, i * 128:(i + 1) * 128, j * 128:(j + 1) * 128] = 0.5 * (
                    corner(f, i, j) + corner(f, j, i).T
                )
        return 0

    lax.fori_loop(0, 2, symmetrize, 0)
    for p in range(8):
        here = slice(p * 128, (p + 1) * 128)
        for f in range(2):
            d_ref[f, :, :128] = l_ref[f, here, here]
            d_ref[f, :, 128:] = eye128()

        def group(g, _):
            for f in range(2):
                rows = d_ref[f, pl.ds(pl.multiple_of(g * 8, 8), 8), :]
                a8, r8 = rows[:, :128], rows[:, 128:]
                turned = pltpu.roll(a8, (128 - g * 8) % 128, 1)
                cols = [jnp.broadcast_to(turned[:, j:j + 1], (8, 128)) for j in range(8)]
                for j in range(8):
                    pivot = jnp.broadcast_to(cols[j][j:j + 1, :], (8, 128))
                    root = lax.rsqrt(pivot)
                    root = root * (1.5 - 0.5 * pivot * root * root)
                    mult = jnp.where(subs > j, cols[j] * root, 0.0)
                    for k in range(j + 1, 8):
                        cols[k] = cols[k] - mult * (cols[k][j:j + 1, :] * root)
                    ua, ur = a8[j:j + 1, :] * root, r8[j:j + 1, :] * root
                    a8 = jnp.where(subs == j, ua, a8 - mult * ua)
                    r8 = jnp.where(subs == j, ur, r8 - mult * ur)
                new = jnp.concatenate([a8, r8], axis=1)
                d_ref[f, pl.ds(pl.multiple_of(g * 8, 8), 8), :] = new
                later = jnp.where(lanes > g * 8 + 7, a8, 0.0)
                d_ref[f] = d_ref[f] - dot_tn(later, new)
            return 0

        lax.fori_loop(0, 16, group, 0)

        def rest(f, _):
            inverse = jnp.where(low, d_ref[f, :, 128:], 0.0)
            l_ref[f, here, here] = jnp.where(low, d_ref[f, :, :128].T, 0.0)
            x_ref[f, here, here] = inverse
            if p > 0:
                done = p * 128
                both = dot_nn(l_ref[f, here, :done], x_ref[f, :done, :done])
                x_ref[f, here, :done] = -dot_nn(inverse, both)
            if p < 7:
                after = (p + 1) * 128
                l_ref[f, here, after:] = jnp.zeros((128, 1024 - after), F32)
                x_ref[f, here, after:] = jnp.zeros((128, 1024 - after), F32)
                l_ref[f, after:, here] = dot_nt(l_ref[f, after:, here], inverse)
                for i in range(p + 1, 8):
                    mine = slice(i * 128, (i + 1) * 128)
                    upto = slice(after, (i + 1) * 128)
                    l_ref[f, mine, upto] = l_ref[f, mine, upto] - dot_nt(
                        l_ref[f, mine, here], l_ref[f, upto, here]
                    )
            return 0

        lax.fori_loop(0, 2, rest, 0)


def factor(pos, corner):
    return pl.pallas_call(
        factor_kernel,
        out_shape=(
            jax.ShapeDtypeStruct((2, 1024, 1024), F32),
            jax.ShapeDtypeStruct((2, 1024, 1024), F32),
        ),
        in_specs=[SM, VM],
        out_specs=(VM, VM),
        scratch_shapes=[pltpu.VMEM((2, 128, 256), F32)],
        compiler_params=params(),
    )(pos, corner)


def left_kernel(pos_ref, a_ref, x_ref, w_ref, own_ref, wide, factor_rows):
    my_col = pos_ref[1]
    for core in range(2):
        for far in range(2):
            column = jnp.bitwise_xor(my_col, core + 2 * far)
            wide[:, pl.ds(pl.multiple_of(column * 256, 256), 256)] = a_ref[core, far, 0]
    factor_rows[...] = dot_nt(wide[...], x_ref[0])
    w_ref[0] = dot_nn(factor_rows[...], x_ref[0])
    own_ref[0] = factor_rows[:, pl.ds(pl.multiple_of(my_col * 256, 256), 256)]


def left(pos, a, inverse):
    return pl.pallas_call(
        left_kernel,
        grid=(2,),
        out_shape=(
            jax.ShapeDtypeStruct((2, 256, 1024), F32),
            jax.ShapeDtypeStruct((2, 256, 256), F32),
        ),
        in_specs=[
            SM,
            pl.BlockSpec((2, 2, 1, 256, 256), lambda f: (0, 0, f, 0, 0)),
            pl.BlockSpec((1, 1024, 1024), lambda f: (f, 0, 0)),
        ],
        out_specs=(
            pl.BlockSpec((1, 256, 1024), lambda f: (f, 0, 0)),
            pl.BlockSpec((1, 256, 256), lambda f: (f, 0, 0)),
        ),
        scratch_shapes=[pltpu.VMEM((256, 1024), F32), pltpu.VMEM((256, 1024), F32)],
        compiler_params=params(),
    )(pos, a, inverse)


def schur_kernel(pos_ref, front_ref, w_ref, own_ref, lo_ref, hi_ref, out_ref, head):
    j = pl.program_id(1)
    my_row = pos_ref[0]
    par = my_row % 2

    @pl.when(j == 0)
    def _():
        for h in range(2):
            out_ref[0, pl.ds(h, 256, stride=16), :] = own_ref[0, :, h * 128:(h + 1) * 128]

    @pl.when((j > 0) & (my_row >= 4))
    def _():
        for h in range(2):
            y = jnp.bitwise_xor(par, h)
            gone = dot_nn(w_ref[0, :, :512], lo_ref[0, 0, y]) + dot_nn(w_ref[0, :, 512:], hi_ref[0, 0, y])
            at = pl.ds(2 * j + h, 256, stride=16)
            out_ref[0, at, :] = front_ref[0, at, :] - gone

    @pl.when((j > 0) & (my_row < 4))
    def _():
        for h in range(2):
            y = jnp.bitwise_xor(par, h)
            start = pl.multiple_of((my_row % 2) * 256, 256)
            at = pl.ds(2 * j + h, 256, stride=16)

            @pl.when(my_row < 2)
            def _():
                out_ref[0, at, :] = lo_ref[0, 0, y, pl.ds(start, 256), :]

            @pl.when(my_row >= 2)
            def _():
                out_ref[0, at, :] = hi_ref[0, 0, y, pl.ds(start, 256), :]


def schur(pos, front, w, own, lo, hi):
    def where(f, j, pos):
        x, z = f * 2 + j % 2, (pos[1] + 4 - j // 2) % 4
        return (pos[0] // 8 + 4 - x) % 4, ((pos[0] // 2) % 4 + 4 - z) % 4

    def lo_map(f, j, pos):
        x, z = where(f, j, pos)
        return x, z, 0, 0, 0

    def hi_map(f, j, pos):
        x, z = where(f, j, pos)
        return z, x, 0, 0, 0

    return pl.pallas_call(
        schur_kernel,
        grid_spec=pltpu.PrefetchScalarGridSpec(
            num_scalar_prefetch=1,
            grid=(2, 8),
            in_specs=[
                pl.BlockSpec((1, 4096, 128), lambda f, j, pos: (f, 0, 0)),
                pl.BlockSpec((1, 256, 1024), lambda f, j, pos: (f, 0, 0)),
                pl.BlockSpec((1, 256, 256), lambda f, j, pos: (f, 0, 0)),
                pl.BlockSpec((1, 1, 2, 512, 128), lo_map),
                pl.BlockSpec((1, 1, 2, 512, 128), hi_map),
            ],
            out_specs=pl.BlockSpec((1, 4096, 128), lambda f, j, pos: (f, 0, 0)),
            scratch_shapes=[pltpu.VMEM((8, 128), F32)],
        ),
        out_shape=jax.ShapeDtypeStruct((2, 4096, 128), F32),
        compiler_params=params(),
    )(pos, front, w, own, lo, hi)


def turn(axis, by):
    pairs = []
    for x in range(4):
        for z in range(4):
            for y in range(2):
                to = ((x + by) % 4, z) if axis == "x" else (x, (z + by) % 4)
                pairs.append((x * 8 + z * 2 + y, to[0] * 8 + to[1] * 2 + y))
    return pairs


def ring(value, axis):
    forth, back = turn(axis, 1), turn(axis, -1)
    half = value.shape[-2] // 2
    below = lax.ppermute(value, "row", forth)
    above = lax.ppermute(value, "row", back)
    first = lax.ppermute(below[..., :half, :], "row", forth)
    second = lax.ppermute(above[..., half:, :], "row", back)
    return jnp.stack([value, below, jnp.concatenate([first, second], axis=-2), above])


def across(value, pairs, axis):
    return jnp.stack([value, lax.ppermute(value, axis, pairs)])


CORE = [(0, 1), (1, 0), (2, 3), (3, 2)]
FAR = [(0, 2), (2, 0), (1, 3), (3, 1)]
NEAR = [(i, i ^ 1) for i in range(32)]


def shards(contrib, target_rows, diag_shift, pattern):
    my_row = lax.axis_index("row").astype(jnp.int32)
    my_col = lax.axis_index("col").astype(jnp.int32)
    pos = jnp.stack([my_row, my_col])
    diag = diag_shift.reshape(2, 2, 128)
    main, panel, marks = build(pos, target_rows, contrib, diag)
    heads = jnp.swapaxes(marks[:4].reshape(4, 2, 16), 0, 1).reshape(2, 1, 64)
    heads = jnp.broadcast_to(heads, (2, 16, 64)).reshape(32, 64)
    marks = lax.all_to_all(
        jnp.concatenate([marks, heads], axis=1), "row", split_axis=0, concat_axis=0, tiled=True
    )
    panel = lax.all_to_all(panel.reshape(32, 72, 128), "row", split_axis=0, concat_axis=0, tiled=True)
    piece = panel_piece(pos, marks, pattern, panel.reshape(32 * 72, 128))
    moves = [
        (i * 4 + c, i * 4 + ((i // 2) % 4 + c) % 4) for i in range(32) for c in range(4)
    ]
    piece = lax.ppermute(piece, ("row", "col"), moves)
    main = lax.all_to_all(
        main.reshape(128, 128, 128), ("row", "col"), split_axis=0, concat_axis=0, tiled=True
    )
    front, own_left = assemble(pos, marks, pattern, diag, main.reshape(16384, 128))

    pair = across(piece, NEAR, "row")
    lo = ring(ring(pair[:, :512], "z"), "x")
    hi = ring(ring(pair[:, 512:], "x"), "z")

    my_x, my_z = my_row // 8, (my_row // 2) % 4
    z_rel = (my_z + 4 - my_col) % 4
    corner = []
    for f in range(2):
        x_rel = (my_x + 4 - 2 * f) % 4
        low = lax.dynamic_slice(lo, (x_rel, z_rel, 0, 0, 0), (1, 1, 2, 512, 128))
        high = lax.dynamic_slice(hi, (z_rel, x_rel, 0, 0, 0), (1, 1, 2, 512, 128))
        corner.append(jnp.concatenate([low[0, 0], high[0, 0]], axis=1))
    corner = jnp.stack(corner)
    corner = across(across(corner, FAR, "col"), CORE, "col")
    lower, inverse = factor(pos, corner)
    lefts = across(across(own_left, FAR, "col"), CORE, "col")
    w, own = left(pos, lefts, inverse)
    head = lax.dynamic_slice(lower, (0, jnp.minimum(my_row, 3) * 256, my_col * 256), (2, 256, 256))
    own = jnp.where(my_row < 4, head, own)
    result = schur(pos, front, w, own, lo, hi)
    return result.reshape(2, 1, 1, 256, 8, 1, 256)


def solution(mesh):
    in_specs = (P(None, "row", "col"), P(None, "row"), P(None, None, "row", None), P())
    out_specs = P(None, None, "row", None, None, "col", None)
    return jax.shard_map(shards, mesh=mesh, in_specs=in_specs, out_specs=out_specs, check_vma=False)
```

```python
import jax
import jax.numpy as jnp
from jax import lax
from jax.experimental import pallas as pl
from jax.experimental.pallas import tpu as pltpu
from jax.sharding import PartitionSpec as P

F = 8192
P_SIZE = 1024
BS = 256
HI = lax.Precision.HIGHEST
VM = pl.BlockSpec(memory_space=pltpu.VMEM)
SM = pl.BlockSpec(memory_space=pltpu.SMEM)
F32 = jnp.float32


def params():
    return pltpu.CompilerParams(vmem_limit_bytes=60 * 1024 * 1024)


def dot_nn(a, b):
    return lax.dot_general(a, b, (((1,), (0,)), ((), ())), precision=HI, preferred_element_type=F32)


def dot_nt(a, b):
    return lax.dot_general(a, b, (((1,), (1,)), ((), ())), precision=HI, preferred_element_type=F32)


def dot_tn(a, b):
    return lax.dot_general(a, b, (((0,), (0,)), ((), ())), precision=HI, preferred_element_type=F32)


def head_kernel(pos_ref, t_ref, x_ref, diag_ref, panel_ref, marks_ref, slots_ref, cnt):
    my_col = pos_ref[1]

    def clear(i, _):
        cnt[i] = 0
        for k in range(16):
            marks_ref[i // 2, (i % 2) * 16 + k] = 256
        return 0

    lax.fori_loop(0, 64, clear, 0)
    for i in range(32):
        panel_ref[pl.ds(i * 72 + 64, 2), :] = diag_ref[i // 16]

    def place_rows(group, _):
        first = pl.multiple_of(group * 8, 8)
        for f in range(2):
            for k in range(8):
                target = t_ref[f, first + k]
                owner = target // 256
                slot = cnt[f * 32 + owner]
                cnt[f * 32 + owner] = slot + 1
                marks_ref[owner, f * 16 + slot] = target % 256
                slots_ref[f, first + k] = owner * 128 + slot

                @pl.when(owner < 4)
                def _():
                    for j in range(16):
                        u, c, h = j // 8, (j // 2) % 4, j % 2
                        q = (c - my_col + 4) % 4
                        dest = f * 16 + u * 8 + q * 2 + h
                        panel_ref[pl.ds(dest * 72 + owner * 16 + slot, 1), :] = (
                            x_ref[f, pl.ds(first, 8), j * 128:(j + 1) * 128][k:k + 1, :]
                        )

        return 0

    lax.fori_loop(0, 32, place_rows, 0)


def build_head(pos, targets, contrib, diag):
    return pl.pallas_call(
        head_kernel,
        out_shape=(
            jax.ShapeDtypeStruct((32 * 72, 128), F32),
            jax.ShapeDtypeStruct((32, 32), jnp.int32),
            jax.ShapeDtypeStruct((2, 256), jnp.int32),
        ),
        in_specs=[SM, SM, VM, VM],
        out_specs=(VM, SM, SM),
        scratch_shapes=[pltpu.SMEM((64,), jnp.int32)],
        compiler_params=params(),
    )(pos, targets, contrib, diag)


def main_kernel(slots_ref, x_ref, main_ref, buf):
    for f in range(2):
        for j in range(16):
            block, half = j // 2, j % 2
            place = (block % 4) * 4 + (block // 4) * 2 + half
            buf[pl.ds(f * 4096 + place, 256, stride=16), :] = x_ref[f, :, j * 128:(j + 1) * 128]

    def place_row(i, _):
        for f in range(2):
            at = slots_ref[f, i]
            source = (f * 256 + i) * 16
            for c in range(4):
                main_ref[pl.ds((at + (c * 2 + f) * 16) * 4, 4), :] = buf[pl.ds(source + c * 4, 4), :]
        return 0

    lax.fori_loop(0, 256, place_row, 0, unroll=2)


def build_main(slots, contrib):
    return pl.pallas_call(
        main_kernel,
        out_shape=jax.ShapeDtypeStruct((16384, 128), F32),
        in_specs=[SM, VM],
        out_specs=VM,
        scratch_shapes=[pltpu.VMEM((8192, 128), F32)],
        compiler_params=params(),
    )(slots, contrib)


def eye128():
    return (
        lax.broadcasted_iota(jnp.int32, (128, 128), 0) == lax.broadcasted_iota(jnp.int32, (128, 128), 1)
    ).astype(F32)


def panel_kernel(pos_ref, marks_ref, pattern_ref, x_ref, out_ref, acc):
    my_row, my_col = pos_ref[0], pos_ref[1]
    f, u, q, h = my_row // 16, (my_row // 8) % 2, (my_row // 2) % 4, my_row % 2
    block = 8 * my_col + u * 4 + (q + my_col) % 4
    acc[...] = jnp.zeros_like(acc)

    def source(s, _):
        def step(k, _):
            rows = [n * 264 + marks_ref[s, 32 + n * 16 + k] for n in range(4)]
            new = [
                acc[pl.ds(rows[n], 1), :] + x_ref[pl.ds(s * 72 + n * 16 + k, 1), :] for n in range(4)
            ]
            for n in range(4):
                acc[pl.ds(rows[n], 1), :] = new[n]
            return 0

        return lax.fori_loop(0, 16, step, 0, unroll=4)

    lax.fori_loop(0, 32, source, 0)
    scale = jnp.where(block >= 4, pattern_ref[f, block], 1).astype(F32)
    for n in range(4):
        out_ref[pl.ds(n * 256, 256), :] = acc[n * 264:n * 264 + 256, :] * scale

    @pl.when(block < 4)
    def _():
        start = pl.multiple_of(block * 256 + h * 128, 128)
        shift = x_ref[pl.ds(block * 72 + 64 + h, 1), :]
        out_ref[pl.ds(start, 128), :] += eye128() * shift


def panel_piece(pos, marks, pattern, received):
    return pl.pallas_call(
        panel_kernel,
        out_shape=jax.ShapeDtypeStruct((1024, 128), F32),
        in_specs=[SM, SM, SM, VM],
        out_specs=VM,
        scratch_shapes=[pltpu.VMEM((1056, 128), F32)],
        compiler_params=params(),
    )(pos, marks, pattern, received)


SRCS = 8


def assemble_kernel(pos_ref, marks_ref, pattern_ref, diag_ref, x_ref, out_ref, left_ref, acc):
    step = pl.program_id(0)
    my_row, my_col = pos_ref[0], pos_ref[1]

    @pl.when(step == 0)
    def _():
        acc[...] = jnp.zeros_like(acc)

    def source(s, _):
        def slot(k, _):
            for f in range(2):
                mark = marks_ref[step * SRCS + s, f * 16 + k]

                @pl.when(mark < 256)
                def _():
                    for c in range(4):
                        piece = x_ref[pl.ds((((s * 4 + c) * 2 + f) * 16 + k) * 4, 4), :]
                        acc[f, pl.ds(mark * 16 + c * 4, 4), :] += piece

            return 0

        return lax.fori_loop(0, 16, slot, 0)

    lax.fori_loop(0, SRCS, source, 0)

    @pl.when(step == pl.num_programs(0) - 1)
    def _():
        for f in range(2):
            scale = jnp.where(my_row >= 4, pattern_ref[f, my_row], 1).astype(F32)

            @pl.when(my_row % 4 == my_col)
            def _():
                for h in range(2):
                    at = pl.ds(h * 2048 + (my_row // 4) * 2 + h, 128, stride=16)
                    acc[f, at, :] += eye128() * diag_ref[f, h:h + 1, :]

            for h in range(2):
                left_ref[f, :, h * 128:(h + 1) * 128] = acc[f, pl.ds(h, 256, stride=16), :] * scale
            out_ref[f] = acc[f]


def assemble(pos, marks, pattern, diag, received):
    chunk = SRCS * 512
    return pl.pallas_call(
        assemble_kernel,
        grid=(32 // SRCS,),
        out_shape=(
            jax.ShapeDtypeStruct((2, 4096, 128), F32),
            jax.ShapeDtypeStruct((2, 256, 256), F32),
        ),
        in_specs=[SM, SM, SM, VM, pl.BlockSpec((chunk, 128), lambda s: (s, 0))],
        out_specs=(
            pl.BlockSpec((2, 4096, 128), lambda s: (0, 0, 0)),
            pl.BlockSpec((2, 256, 256), lambda s: (0, 0, 0)),
        ),
        scratch_shapes=[pltpu.VMEM((2, 4096, 128), F32)],
        compiler_params=params(),
    )(pos, marks, pattern, diag, received)


def factor_steps(steps, l_ref, x_ref, d_ref):
    lanes = lax.broadcasted_iota(jnp.int32, (8, 128), 1)
    subs = lax.broadcasted_iota(jnp.int32, (8, 128), 0)
    low = lax.broadcasted_iota(jnp.int32, (128, 128), 0) >= lax.broadcasted_iota(jnp.int32, (128, 128), 1)

    for p in steps:
        here = slice(p * 128, (p + 1) * 128)
        d_ref[:, :128] = l_ref[here, here]
        d_ref[:, 128:] = eye128()

        def group(g, _):
            rows = d_ref[pl.ds(pl.multiple_of(g * 8, 8), 8), :]
            a8, r8 = rows[:, :128], rows[:, 128:]
            turned = pltpu.roll(a8, (128 - g * 8) % 128, 1)
            cols = [jnp.broadcast_to(turned[:, j:j + 1], (8, 128)) for j in range(8)]
            for j in range(8):
                pivot = jnp.broadcast_to(cols[j][j:j + 1, :], (8, 128))
                root = lax.rsqrt(pivot)
                root = root * (1.5 - 0.5 * pivot * root * root)
                mult = jnp.where(subs > j, cols[j] * root, 0.0)
                for k in range(j + 1, 8):
                    cols[k] = cols[k] - mult * (cols[k][j:j + 1, :] * root)
                ua, ur = a8[j:j + 1, :] * root, r8[j:j + 1, :] * root
                a8 = jnp.where(subs == j, ua, a8 - mult * ua)
                r8 = jnp.where(subs == j, ur, r8 - mult * ur)
            new = jnp.concatenate([a8, r8], axis=1)
            d_ref[pl.ds(pl.multiple_of(g * 8, 8), 8), :] = new
            later = jnp.where(lanes > g * 8 + 7, a8, 0.0)
            d_ref[...] = d_ref[...] - dot_tn(later, new)
            return 0

        lax.fori_loop(0, 16, group, 0)
        inverse = jnp.where(low, d_ref[:, 128:], 0.0)
        l_ref[here, here] = jnp.where(low, d_ref[:, :128].T, 0.0)
        x_ref[here, here] = inverse
        if p > 0:
            done = p * 128
            both = dot_nn(l_ref[here, :done], x_ref[:done, :done])
            x_ref[here, :done] = -dot_nn(inverse, both)
        if p < 7:
            after = (p + 1) * 128
            l_ref[here, after:] = jnp.zeros((128, 1024 - after), F32)
            x_ref[here, after:] = jnp.zeros((128, 1024 - after), F32)
            l_ref[after:, here] = dot_nt(l_ref[after:, here], inverse)
            for i in range(p + 1, 8):
                mine = slice(i * 128, (i + 1) * 128)
                upto = slice(after, (i + 1) * 128)
                l_ref[mine, upto] = l_ref[mine, upto] - dot_nt(l_ref[mine, here], l_ref[upto, here])


CUT = 6


def factor_start_kernel(pos_ref, c_ref, l_ref, x_ref, d_ref):
    my_row, my_col = pos_ref[0], pos_ref[1]

    def corner(rows, block):
        other = jnp.bitwise_xor(block // 2, my_col)
        return c_ref[other // 2, other % 2, jnp.bitwise_xor(block % 2, my_row % 2), pl.ds(rows * 128, 128), :]

    for i in range(8):
        for j in range(i + 1):
            l_ref[i * 128:(i + 1) * 128, j * 128:(j + 1) * 128] = 0.5 * (corner(i, j) + corner(j, i).T)
    factor_steps(range(CUT), l_ref, x_ref, d_ref)


def factor_end_kernel(l_in, x_in, l_ref, x_ref, d_ref):
    l_ref[...] = l_in[...]
    x_ref[:CUT * 128, :] = x_in[:CUT * 128, :]
    factor_steps(range(CUT, 8), l_ref, x_ref, d_ref)


def factor(kernel, specs, flops, *operands):
    whole = jax.ShapeDtypeStruct((1024, 1024), F32)
    return pl.pallas_call(
        kernel,
        out_shape=(whole, whole),
        in_specs=specs,
        out_specs=(VM, VM),
        scratch_shapes=[pltpu.VMEM((128, 256), F32)],
        compiler_params=params(),
        cost_estimate=pl.CostEstimate(flops=flops, bytes_accessed=12 * 2**20, transcendentals=0),
    )(*operands)


def left_kernel(pos_ref, a_ref, x_ref, head_ref, w_ref, wide, rows):
    my_row, my_col = pos_ref[0], pos_ref[1]
    for far in range(2):
        for core in range(2):
            column = jnp.bitwise_xor(my_col, core + 2 * far)
            wide[:, pl.ds(pl.multiple_of(column * 256, 256), 256)] = a_ref[far, core]
    rows[...] = dot_nt(wide[...], x_ref[...])
    w_ref[:, :1024] = dot_nn(rows[...], x_ref[...])

    @pl.when(my_row < 4)
    def _():
        rows[...] = head_ref[...]

    for core in range(2):
        column = pl.multiple_of(jnp.bitwise_xor(my_col, core) * 256, 256)
        w_ref[:, 1024 + core * 256:1280 + core * 256] = rows[:, pl.ds(column, 256)]


def left(pos, a, inverse, lower):
    return pl.pallas_call(
        left_kernel,
        grid_spec=pltpu.PrefetchScalarGridSpec(
            num_scalar_prefetch=1,
            grid=(1,),
            in_specs=[
                pl.BlockSpec((2, 2, 256, 256), lambda i, pos: (0, 0, 0, 0)),
                pl.BlockSpec((1024, 1024), lambda i, pos: (0, 0)),
                pl.BlockSpec((256, 1024), lambda i, pos: (jnp.minimum(pos[0], 3), 0)),
            ],
            out_specs=pl.BlockSpec((256, 1536), lambda i, pos: (0, 0)),
            scratch_shapes=[pltpu.VMEM((256, 1024), F32), pltpu.VMEM((256, 1024), F32)],
        ),
        out_shape=jax.ShapeDtypeStruct((256, 1536), F32),
        compiler_params=params(),
    )(pos, a, inverse, lower)


def schur_kernel(pos_ref, front_ref, w_ref, lo_ref, hi_ref, out_ref):
    j = pl.program_id(1)
    my_row = pos_ref[0]
    par = my_row % 2

    @pl.when(j == 0)
    def _():
        for h in range(2):
            out_ref[0, pl.ds(h, 256, stride=16), :] = w_ref[0, :, 1024 + h * 128:1152 + h * 128]

    @pl.when((j > 0) & (my_row >= 4))
    def _():
        for h in range(2):
            y = jnp.bitwise_xor(par, h)
            gone = dot_nn(w_ref[0, :, :512], lo_ref[0, 0, y]) + dot_nn(w_ref[0, :, 512:1024], hi_ref[0, 0, y])
            at = pl.ds(2 * j + h, 256, stride=16)
            out_ref[0, at, :] = front_ref[0, at, :] - gone

    @pl.when((j > 0) & (my_row < 4))
    def _():
        for h in range(2):
            y = jnp.bitwise_xor(par, h)
            start = pl.multiple_of((my_row % 2) * 256, 256)
            at = pl.ds(2 * j + h, 256, stride=16)

            @pl.when(my_row < 2)
            def _():
                out_ref[0, at, :] = lo_ref[0, 0, y, pl.ds(start, 256), :]

            @pl.when(my_row >= 2)
            def _():
                out_ref[0, at, :] = hi_ref[0, 0, y, pl.ds(start, 256), :]


def schur(pos, front, w, lo, hi):
    def where(f, j, pos):
        x, z = f * 2 + j % 2, (pos[1] + 4 - j // 2) % 4
        return (pos[0] // 8 + 4 - x) % 4, ((pos[0] // 2) % 4 + 4 - z) % 4

    def lo_map(f, j, pos):
        x, z = where(f, j, pos)
        return x, z, 0, 0, 0

    def hi_map(f, j, pos):
        x, z = where(f, j, pos)
        return z, x, 0, 0, 0

    return pl.pallas_call(
        schur_kernel,
        grid_spec=pltpu.PrefetchScalarGridSpec(
            num_scalar_prefetch=1,
            grid=(2, 8),
            in_specs=[
                pl.BlockSpec((1, 4096, 128), lambda f, j, pos: (f, 0, 0)),
                pl.BlockSpec(
                    (1, 256, 1280), lambda f, j, pos: (jnp.bitwise_xor(f, pos[1] % 2), 0, 0)
                ),
                pl.BlockSpec((1, 1, 2, 512, 128), lo_map),
                pl.BlockSpec((1, 1, 2, 512, 128), hi_map),
            ],
            out_specs=pl.BlockSpec((1, 4096, 128), lambda f, j, pos: (f, 0, 0)),
        ),
        out_shape=jax.ShapeDtypeStruct((2, 4096, 128), F32),
        compiler_params=params(),
    )(pos, front, w, lo, hi)


def turn(axis, by):
    pairs = []
    for x in range(4):
        for z in range(4):
            for y in range(2):
                to = ((x + by) % 4, z) if axis == "x" else (x, (z + by) % 4)
                pairs.append((x * 8 + z * 2 + y, to[0] * 8 + to[1] * 2 + y))
    return pairs


def ring(value, axis):
    forth, back = turn(axis, 1), turn(axis, -1)
    half = value.shape[-2] // 2
    below = lax.ppermute(value, "row", forth)
    above = lax.ppermute(value, "row", back)
    first = lax.ppermute(below[..., :half, :], "row", forth)
    second = lax.ppermute(above[..., half:, :], "row", back)
    return jnp.stack([value, below, jnp.concatenate([first, second], axis=-2), above])


def across(value, pairs, axis):
    return jnp.stack([value, lax.ppermute(value, axis, pairs)])


CORE = [(0, 1), (1, 0), (2, 3), (3, 2)]
FAR = [(0, 2), (2, 0), (1, 3), (3, 1)]
NEAR = [(i, i ^ 1) for i in range(32)]


def own_front(value, my_core):
    kept = lax.dynamic_index_in_dim(value, my_core, 0, keepdims=False)
    given = lax.dynamic_index_in_dim(value, 1 - my_core, 0, keepdims=False)
    return across(jnp.stack([kept, lax.ppermute(given, "col", CORE)]), FAR, "col")


def shards(contrib, target_rows, diag_shift, pattern):
    my_row = lax.axis_index("row").astype(jnp.int32)
    my_col = lax.axis_index("col").astype(jnp.int32)
    my_core = my_col % 2
    pos = jnp.stack([my_row, my_col])
    diag = diag_shift.reshape(2, 2, 128)
    panel, marks, slots = build_head(pos, target_rows, contrib, diag)
    heads = jnp.swapaxes(marks[:4].reshape(4, 2, 16), 0, 1).reshape(2, 1, 64)
    heads = jnp.broadcast_to(heads, (2, 16, 64)).reshape(32, 64)
    marks = jnp.concatenate([marks, heads, heads[:, :32]], axis=1).astype(F32)
    panel = panel.reshape(32, 72, 128).at[:, 66, :].set(marks)
    panel = lax.all_to_all(panel, "row", split_axis=0, concat_axis=0, tiled=True)
    marks = panel[:, 66, :96].astype(jnp.int32)
    piece = panel_piece(pos, marks, pattern, panel.reshape(32 * 72, 128))
    slots, piece = lax.optimization_barrier((slots, piece))
    main = build_main(slots, contrib)
    moves = [
        (i * 4 + c, i * 4 + ((i // 2) % 4 + c) % 4) for i in range(32) for c in range(4)
    ]
    piece = lax.ppermute(piece, ("row", "col"), moves)
    pair = across(piece, NEAR, "row")
    lo = ring(ring(pair[:, :512], "z"), "x")
    hi = ring(ring(pair[:, 512:], "x"), "z")

    my_x, my_z = my_row // 8, (my_row // 2) % 4
    z_rel = (my_z + 4 - my_col) % 4
    corner = []
    for f in range(2):
        x_rel = (my_x + 4 - 2 * f) % 4
        low = lax.dynamic_slice(lo, (x_rel, z_rel, 0, 0, 0), (1, 1, 2, 512, 128))
        high = lax.dynamic_slice(hi, (z_rel, x_rel, 0, 0, 0), (1, 1, 2, 512, 128))
        corner.append(jnp.concatenate([low[0, 0], high[0, 0]], axis=1))
    corner = own_front(jnp.stack(corner), my_core)
    corner, main = lax.optimization_barrier((corner, main))
    main = lax.all_to_all(
        main.reshape(128, 128, 128), ("row", "col"), split_axis=0, concat_axis=0, tiled=True
    )
    lower, inverse = factor(factor_start_kernel, [SM, VM], 9 * 10**10, pos, corner)
    main, lower = lax.optimization_barrier((main, lower))
    front, own_left = assemble(pos, marks, pattern, diag, main.reshape(16384, 128))
    lefts = own_front(own_left, my_core)
    lower, inverse = factor(factor_end_kernel, [VM, VM], 3 * 10**10, lower, inverse)
    w = left(pos, lefts, inverse, lower)
    kept = w[:, :1280]
    given = jnp.concatenate([w[:, :1024], w[:, 1280:]], axis=1)
    w = jnp.stack([kept, lax.ppermute(given, "col", CORE)])
    result = schur(pos, front, w, lo, hi)
    return result.reshape(2, 1, 1, 256, 8, 1, 256)


def solution(mesh):
    in_specs = (P(None, "row", "col"), P(None, "row"), P(None, None, "row", None), P())
    out_specs = P(None, None, "row", None, None, "col", None)
    return jax.shard_map(shards, mesh=mesh, in_specs=in_specs, out_specs=out_specs, check_vma=False)
```

```python
import jax
import jax.numpy as jnp
from jax import lax
from jax.experimental import pallas as pl
from jax.experimental.pallas import tpu as pltpu
from jax.sharding import PartitionSpec as P

F = 8192
P_SIZE = 1024
BS = 256
HI = lax.Precision.HIGHEST
VM = pl.BlockSpec(memory_space=pltpu.VMEM)
SM = pl.BlockSpec(memory_space=pltpu.SMEM)
F32 = jnp.float32


def params():
    return pltpu.CompilerParams(vmem_limit_bytes=60 * 1024 * 1024)


def dot_nn(a, b):
    return lax.dot_general(a, b, (((1,), (0,)), ((), ())), precision=HI, preferred_element_type=F32)


def dot_nt(a, b):
    return lax.dot_general(a, b, (((1,), (1,)), ((), ())), precision=HI, preferred_element_type=F32)


def dot_tn(a, b):
    return lax.dot_general(a, b, (((0,), (0,)), ((), ())), precision=HI, preferred_element_type=F32)


def head_kernel(pos_ref, t_ref, x_ref, diag_ref, panel_ref, marks_ref, slots_ref, cnt):
    my_col = pos_ref[1]

    def clear(i, _):
        cnt[i] = 0
        for k in range(16):
            marks_ref[i // 2, (i % 2) * 16 + k] = 256
        return 0

    lax.fori_loop(0, 64, clear, 0)
    for i in range(32):
        panel_ref[pl.ds(i * 72 + 64, 2), :] = diag_ref[i // 16]

    def place_rows(group, _):
        first = pl.multiple_of(group * 8, 8)
        for f in range(2):
            for k in range(8):
                target = t_ref[f, first + k]
                owner = lax.shift_right_logical(target, 8)
                slot = cnt[f * 32 + owner]
                cnt[f * 32 + owner] = slot + 1
                marks_ref[owner, f * 16 + slot] = jnp.bitwise_and(target, 255)
                slots_ref[f, first + k] = owner * 128 + slot

                @pl.when(owner < 4)
                def _():
                    for j in range(16):
                        u, c, h = j // 8, (j // 2) % 4, j % 2
                        q = jnp.bitwise_and(c + 4 - my_col, 3)
                        dest = f * 16 + u * 8 + q * 2 + h
                        panel_ref[pl.ds(dest * 72 + owner * 16 + slot, 1), :] = (
                            x_ref[f, pl.ds(first, 8), j * 128:(j + 1) * 128][k:k + 1, :]
                        )

        return 0

    lax.fori_loop(0, 32, place_rows, 0)


def build_head(pos, targets, contrib, diag):
    return pl.pallas_call(
        head_kernel,
        out_shape=(
            jax.ShapeDtypeStruct((32 * 72, 128), F32),
            jax.ShapeDtypeStruct((32, 32), jnp.int32),
            jax.ShapeDtypeStruct((2, 256), jnp.int32),
        ),
        in_specs=[SM, SM, VM, VM],
        out_specs=(VM, SM, SM),
        scratch_shapes=[pltpu.SMEM((64,), jnp.int32)],
        compiler_params=params(),
    )(pos, targets, contrib, diag)


def main_kernel(slots_ref, x_ref, main_ref, buf):
    for f in range(2):
        for j in range(16):
            block, half = j // 2, j % 2
            place = (block % 4) * 4 + (block // 4) * 2 + half
            buf[pl.ds(f * 4096 + place, 256, stride=16), :] = x_ref[f, :, j * 128:(j + 1) * 128]

    def place_row(i, _):
        for f in range(2):
            at = slots_ref[f, i]
            source = (f * 256 + i) * 16
            for c in range(4):
                main_ref[pl.ds((at + (c * 2 + f) * 16) * 4, 4), :] = buf[pl.ds(source + c * 4, 4), :]
        return 0

    lax.fori_loop(0, 256, place_row, 0, unroll=2)


def build_main(slots, contrib):
    return pl.pallas_call(
        main_kernel,
        out_shape=jax.ShapeDtypeStruct((16384, 128), F32),
        in_specs=[SM, VM],
        out_specs=VM,
        scratch_shapes=[pltpu.VMEM((8192, 128), F32)],
        compiler_params=params(),
        cost_estimate=pl.CostEstimate(flops=10**10, bytes_accessed=2**23, transcendentals=0),
    )(slots, contrib)


def eye128():
    return (
        lax.broadcasted_iota(jnp.int32, (128, 128), 0) == lax.broadcasted_iota(jnp.int32, (128, 128), 1)
    ).astype(F32)


def panel_kernel(pos_ref, marks_ref, pattern_ref, x_ref, out_ref, acc):
    my_row, my_col = pos_ref[0], pos_ref[1]
    f, u, q, h = my_row // 16, (my_row // 8) % 2, (my_row // 2) % 4, my_row % 2
    block = 8 * my_col + u * 4 + (q + my_col) % 4
    acc[...] = jnp.zeros_like(acc)

    def source(s, _):
        def step(k, _):
            rows = [n * 264 + marks_ref[s, 32 + n * 16 + k] for n in range(4)]
            new = [
                acc[pl.ds(rows[n], 1), :] + x_ref[pl.ds(s * 72 + n * 16 + k, 1), :] for n in range(4)
            ]
            for n in range(4):
                acc[pl.ds(rows[n], 1), :] = new[n]
            return 0

        return lax.fori_loop(0, 16, step, 0, unroll=4)

    lax.fori_loop(0, 32, source, 0)
    scale = jnp.where(block >= 4, pattern_ref[f, block], 1).astype(F32)
    for n in range(4):
        out_ref[pl.ds(n * 256, 256), :] = acc[n * 264:n * 264 + 256, :] * scale

    @pl.when(block < 4)
    def _():
        start = pl.multiple_of(block * 256 + h * 128, 128)
        shift = x_ref[pl.ds(block * 72 + 64 + h, 1), :]
        out_ref[pl.ds(start, 128), :] += eye128() * shift


def panel_piece(pos, marks, pattern, received):
    return pl.pallas_call(
        panel_kernel,
        out_shape=jax.ShapeDtypeStruct((1024, 128), F32),
        in_specs=[SM, SM, SM, VM],
        out_specs=VM,
        scratch_shapes=[pltpu.VMEM((1056, 128), F32)],
        compiler_params=params(),
    )(pos, marks, pattern, received)


SRCS = 8


def assemble_kernel(pos_ref, marks_ref, pattern_ref, diag_ref, x_ref, out_ref, left_ref, acc):
    step = pl.program_id(0)
    my_row, my_col = pos_ref[0], pos_ref[1]

    @pl.when(step == 0)
    def _():
        acc[...] = jnp.zeros_like(acc)

    def source(s, _):
        def slot(k, _):
            for f in range(2):
                mark = marks_ref[step * SRCS + s, f * 16 + k]

                @pl.when(mark < 256)
                def _():
                    for c in range(4):
                        piece = x_ref[pl.ds((((s * 4 + c) * 2 + f) * 16 + k) * 4, 4), :]
                        acc[f, pl.ds(mark * 16 + c * 4, 4), :] += piece

            return 0

        return lax.fori_loop(0, 16, slot, 0)

    lax.fori_loop(0, SRCS, source, 0)

    @pl.when(step == pl.num_programs(0) - 1)
    def _():
        for f in range(2):
            scale = jnp.where(my_row >= 4, pattern_ref[f, my_row], 1).astype(F32)

            @pl.when(my_row % 4 == my_col)
            def _():
                for h in range(2):
                    at = pl.ds(h * 2048 + (my_row // 4) * 2 + h, 128, stride=16)
                    acc[f, at, :] += eye128() * diag_ref[f, h:h + 1, :]

            for h in range(2):
                left_ref[f, :, h * 128:(h + 1) * 128] = acc[f, pl.ds(h, 256, stride=16), :] * scale
            out_ref[f] = acc[f]


def assemble(pos, marks, pattern, diag, received):
    chunk = SRCS * 512
    return pl.pallas_call(
        assemble_kernel,
        grid=(32 // SRCS,),
        out_shape=(
            jax.ShapeDtypeStruct((2, 4096, 128), F32),
            jax.ShapeDtypeStruct((2, 256, 256), F32),
        ),
        in_specs=[SM, SM, SM, VM, pl.BlockSpec((chunk, 128), lambda s: (s, 0))],
        out_specs=(
            pl.BlockSpec((2, 4096, 128), lambda s: (0, 0, 0)),
            pl.BlockSpec((2, 256, 256), lambda s: (0, 0, 0)),
        ),
        scratch_shapes=[pltpu.VMEM((2, 4096, 128), F32)],
        compiler_params=params(),
        cost_estimate=pl.CostEstimate(flops=10**6, bytes_accessed=2**12, transcendentals=0),
    )(pos, marks, pattern, diag, received)


def factor_steps(steps, l_ref, x_ref, d_ref):
    lanes = lax.broadcasted_iota(jnp.int32, (8, 128), 1)
    subs = lax.broadcasted_iota(jnp.int32, (8, 128), 0)
    low = lax.broadcasted_iota(jnp.int32, (128, 128), 0) >= lax.broadcasted_iota(jnp.int32, (128, 128), 1)

    for p in steps:
        here = slice(p * 128, (p + 1) * 128)
        d_ref[:, :128] = l_ref[here, here]
        d_ref[:, 128:] = eye128()

        def group(g, _):
            rows = d_ref[pl.ds(pl.multiple_of(g * 8, 8), 8), :]
            a8, r8 = rows[:, :128], rows[:, 128:]
            turned = pltpu.roll(a8, (128 - g * 8) % 128, 1)
            cols = [jnp.broadcast_to(turned[:, j:j + 1], (8, 128)) for j in range(8)]
            for j in range(8):
                pivot = jnp.broadcast_to(cols[j][j:j + 1, :], (8, 128))
                root = lax.rsqrt(pivot)
                root = root * (1.5 - 0.5 * pivot * root * root)
                mult = jnp.where(subs > j, cols[j] * root, 0.0)
                for k in range(j + 1, 8):
                    cols[k] = cols[k] - mult * (cols[k][j:j + 1, :] * root)
                ua, ur = a8[j:j + 1, :] * root, r8[j:j + 1, :] * root
                a8 = jnp.where(subs == j, ua, a8 - mult * ua)
                r8 = jnp.where(subs == j, ur, r8 - mult * ur)
            new = jnp.concatenate([a8, r8], axis=1)
            d_ref[pl.ds(pl.multiple_of(g * 8, 8), 8), :] = new
            later = jnp.where(lanes > g * 8 + 7, a8, 0.0)
            d_ref[...] = d_ref[...] - dot_tn(later, new)
            return 0

        lax.fori_loop(0, 16, group, 0)
        inverse = jnp.where(low, d_ref[:, 128:], 0.0)
        l_ref[here, here] = jnp.where(low, d_ref[:, :128].T, 0.0)
        x_ref[here, here] = inverse
        if p > 0:
            done = p * 128
            both = dot_nn(l_ref[here, :done], x_ref[:done, :done])
            x_ref[here, :done] = -dot_nn(inverse, both)
        if p < 7:
            after = (p + 1) * 128
            l_ref[here, after:] = jnp.zeros((128, 1024 - after), F32)
            x_ref[here, after:] = jnp.zeros((128, 1024 - after), F32)
            l_ref[after:, here] = dot_nt(l_ref[after:, here], inverse)
            for i in range(p + 1, 8):
                mine = slice(i * 128, (i + 1) * 128)
                upto = slice(after, (i + 1) * 128)
                l_ref[mine, upto] = l_ref[mine, upto] - dot_nt(l_ref[mine, here], l_ref[upto, here])


def factor_kernel(pos_ref, lo_ref, hi_ref, l_ref, x_ref, d_ref):
    my_z = (pos_ref[0] // 2) % 4

    def corner(rows, block):
        ref = lo_ref if rows < 4 else hi_ref
        return ref[(my_z + 4 - block // 2) % 4, block % 2, (rows % 4) * 128:(rows % 4 + 1) * 128, :]

    for i in range(8):
        for j in range(i + 1):
            l_ref[i * 128:(i + 1) * 128, j * 128:(j + 1) * 128] = 0.5 * (corner(i, j) + corner(j, i).T)
    factor_steps(range(8), l_ref, x_ref, d_ref)


def factor(pos, corner_lo, corner_hi):
    whole = jax.ShapeDtypeStruct((1024, 1024), F32)
    return pl.pallas_call(
        factor_kernel,
        out_shape=(whole, whole),
        in_specs=[SM, VM, VM],
        out_specs=(VM, VM),
        scratch_shapes=[pltpu.VMEM((128, 256), F32)],
        compiler_params=params(),
        cost_estimate=pl.CostEstimate(flops=10**11, bytes_accessed=12 * 2**20, transcendentals=0),
    )(pos, corner_lo, corner_hi)


def left_kernel(pos_ref, a_ref, x_ref, head_ref, w_ref, wide, rows):
    my_row, my_col = pos_ref[0], pos_ref[1]
    for far in range(2):
        for core in range(2):
            column = jnp.bitwise_xor(my_col, core + 2 * far)
            wide[:, pl.ds(pl.multiple_of(column * 256, 256), 256)] = a_ref[far, core]
    rows[...] = dot_nt(wide[...], x_ref[...])
    w_ref[:, :1024] = dot_nn(rows[...], x_ref[...])

    @pl.when(my_row < 4)
    def _():
        rows[...] = head_ref[...]

    for core in range(2):
        column = pl.multiple_of(jnp.bitwise_xor(my_col, core) * 256, 256)
        w_ref[:, 1024 + core * 256:1280 + core * 256] = rows[:, pl.ds(column, 256)]


def left(pos, a, inverse, lower):
    return pl.pallas_call(
        left_kernel,
        grid_spec=pltpu.PrefetchScalarGridSpec(
            num_scalar_prefetch=1,
            grid=(1,),
            in_specs=[
                pl.BlockSpec((2, 2, 256, 256), lambda i, pos: (0, 0, 0, 0)),
                pl.BlockSpec((1024, 1024), lambda i, pos: (0, 0)),
                pl.BlockSpec((256, 1024), lambda i, pos: (jnp.minimum(pos[0], 3), 0)),
            ],
            out_specs=pl.BlockSpec((256, 1536), lambda i, pos: (0, 0)),
            scratch_shapes=[pltpu.VMEM((256, 1024), F32), pltpu.VMEM((256, 1024), F32)],
        ),
        out_shape=jax.ShapeDtypeStruct((256, 1536), F32),
        compiler_params=params(),
        cost_estimate=pl.CostEstimate(flops=10**6, bytes_accessed=2**12, transcendentals=0),
    )(pos, a, inverse, lower)


def schur_kernel(pos_ref, front_ref, w_ref, lo_ref, hi_ref, out_ref):
    j = pl.program_id(1)
    my_row = pos_ref[0]
    par = my_row % 2

    @pl.when(j == 0)
    def _():
        for h in range(2):
            out_ref[0, pl.ds(h, 256, stride=16), :] = w_ref[0, :, 1024 + h * 128:1152 + h * 128]

    @pl.when((j > 0) & (my_row >= 4))
    def _():
        for h in range(2):
            y = jnp.bitwise_xor(par, h)
            gone = dot_nn(w_ref[0, :, :512], lo_ref[0, 0, y]) + dot_nn(w_ref[0, :, 512:1024], hi_ref[0, 0, y])
            at = pl.ds(2 * j + h, 256, stride=16)
            out_ref[0, at, :] = front_ref[0, at, :] - gone

    @pl.when((j > 0) & (my_row < 4))
    def _():
        for h in range(2):
            y = jnp.bitwise_xor(par, h)
            start = pl.multiple_of((my_row % 2) * 256, 256)
            at = pl.ds(2 * j + h, 256, stride=16)

            @pl.when(my_row < 2)
            def _():
                out_ref[0, at, :] = lo_ref[0, 0, y, pl.ds(start, 256), :]

            @pl.when(my_row >= 2)
            def _():
                out_ref[0, at, :] = hi_ref[0, 0, y, pl.ds(start, 256), :]


def schur(pos, front, w, lo, hi):
    def where(f, j, pos):
        x, z = f * 2 + j % 2, (pos[1] + 4 - j // 2) % 4
        return (pos[0] // 8 + 4 - x) % 4, ((pos[0] // 2) % 4 + 4 - z) % 4

    def lo_map(f, j, pos):
        x, z = where(f, j, pos)
        return x, z, 0, 0, 0

    def hi_map(f, j, pos):
        x, z = where(f, j, pos)
        return z, x, 0, 0, 0

    return pl.pallas_call(
        schur_kernel,
        grid_spec=pltpu.PrefetchScalarGridSpec(
            num_scalar_prefetch=1,
            grid=(2, 8),
            in_specs=[
                pl.BlockSpec((1, 4096, 128), lambda f, j, pos: (f, 0, 0)),
                pl.BlockSpec(
                    (1, 256, 1280), lambda f, j, pos: (jnp.bitwise_xor(f, pos[1] % 2), 0, 0)
                ),
                pl.BlockSpec((1, 1, 2, 512, 128), lo_map),
                pl.BlockSpec((1, 1, 2, 512, 128), hi_map),
            ],
            out_specs=pl.BlockSpec((1, 4096, 128), lambda f, j, pos: (f, 0, 0)),
        ),
        out_shape=jax.ShapeDtypeStruct((2, 4096, 128), F32),
        compiler_params=params(),
    )(pos, front, w, lo, hi)


def turn(axis, by):
    pairs = []
    for x in range(4):
        for z in range(4):
            for y in range(2):
                to = ((x + by) % 4, z) if axis == "x" else (x, (z + by) % 4)
                pairs.append((x * 8 + z * 2 + y, to[0] * 8 + to[1] * 2 + y))
    return pairs


def ring(value, axis):
    forth, back = turn(axis, 1), turn(axis, -1)
    half = value.shape[-2] // 2
    below = lax.ppermute(value, "row", forth)
    above = lax.ppermute(value, "row", back)
    first = lax.ppermute(below[..., :half, :], "row", forth)
    second = lax.ppermute(above[..., half:, :], "row", back)
    return jnp.stack([value, below, jnp.concatenate([first, second], axis=-2), above])


def across(value, pairs, axis):
    return jnp.stack([value, lax.ppermute(value, axis, pairs)])


CORE = [(0, 1), (1, 0), (2, 3), (3, 2)]
FAR = [(0, 2), (2, 0), (1, 3), (3, 1)]
NEAR = [(i, i ^ 1) for i in range(32)]


def own_front(value, my_core):
    kept = lax.dynamic_index_in_dim(value, my_core, 0, keepdims=False)
    given = lax.dynamic_index_in_dim(value, 1 - my_core, 0, keepdims=False)
    return across(jnp.stack([kept, lax.ppermute(given, "col", CORE)]), FAR, "col")


def device(x, z, y, core):
    return (x * 8 + z * 2 + y % 2) * 4 + (y // 2) * 2 + core


def corner_columns(piece, my_x, my_z, my_y, my_core):
    both = ("row", "col")
    got = []
    for k in range(4):
        pairs = [
            (device(2 * f, z, h, 0), device(2 * f, z, (h + k) % 4, f))
            for f in range(2) for z in range(4) for h in range(2)
        ]
        got.append(lax.ppermute(piece, both, pairs))
    got = jnp.stack(got)
    pair = jnp.stack(
        [lax.dynamic_index_in_dim(got, (my_y + 4 - h) % 4, 0, keepdims=False) for h in range(2)]
    )
    away = (my_x + 4 - 2 * my_core) % 4

    def spread_x(value):
        half = value.shape[-2] // 2

        def moved(part, start, by):
            pairs = [
                (device((2 * core + start) % 4, z, y, core), device((2 * core + start + by) % 4, z, y, core))
                for z in range(4) for y in range(4) for core in range(2)
            ]
            return lax.ppermute(part, both, pairs)

        below, above = moved(value, 0, 1), moved(value, 0, -1)
        far = jnp.concatenate(
            [moved(below[..., :half, :], 1, 1), moved(above[..., half:, :], 3, -1)], axis=-2
        )
        return jnp.where(away == 0, value, jnp.where(away == 1, below, jnp.where(away == 3, above, far)))

    def ring_z(value, xs):
        half = value.shape[-2] // 2

        def moved(part, by):
            pairs = [
                (device(x, z, y, core), device(x, (z + by) % 4, y, core))
                for z in range(4) for y in range(4) for core in range(2) for x in xs(core)
            ]
            return lax.ppermute(part, both, pairs)

        below, above = moved(value, 1), moved(value, -1)
        far = jnp.concatenate([moved(below[..., :half, :], 1), moved(above[..., half:, :], -1)], axis=-2)
        return jnp.stack([value, below, far, above])

    lo = spread_x(ring_z(pair[:, :512], lambda core: [2 * core]))
    hi = ring_z(spread_x(pair[:, 512:]), lambda core: range(4))
    return lo, hi


def shards(contrib, target_rows, diag_shift, pattern):
    my_row = lax.axis_index("row").astype(jnp.int32)
    my_col = lax.axis_index("col").astype(jnp.int32)
    my_core = my_col % 2
    my_x, my_z, my_y = my_row // 8, (my_row // 2) % 4, (my_col // 2) * 2 + my_row % 2
    pos = jnp.stack([my_row, my_col])
    diag = diag_shift.reshape(2, 2, 128)
    panel, marks, slots = build_head(pos, target_rows, contrib, diag)
    heads = jnp.swapaxes(marks[:4].reshape(4, 2, 16), 0, 1).reshape(2, 1, 64)
    heads = jnp.broadcast_to(heads, (2, 16, 64)).reshape(32, 64)
    marks = jnp.concatenate([marks, heads, heads[:, :32]], axis=1).astype(F32)
    panel = panel.reshape(32, 72, 128).at[:, 66, :].set(marks)
    panel = lax.all_to_all(panel, "row", split_axis=0, concat_axis=0, tiled=True)
    marks = panel[:, 66, :96].astype(jnp.int32)
    piece = panel_piece(pos, marks, pattern, panel.reshape(32 * 72, 128))
    slots, piece = lax.optimization_barrier((slots, piece))
    main = build_main(slots, contrib)
    corner_lo, corner_hi = corner_columns(piece, my_x, my_z, my_y, my_core)
    moves = [
        (i * 4 + c, i * 4 + ((i // 2) % 4 + c) % 4) for i in range(32) for c in range(4)
    ]
    pair = across(lax.ppermute(piece, ("row", "col"), moves), NEAR, "row")
    lo, hi = ring(pair[:, :512], "z"), ring(pair[:, 512:], "x")
    corner_lo, corner_hi, main, lo, hi = lax.optimization_barrier((corner_lo, corner_hi, main, lo, hi))
    main = lax.all_to_all(
        main.reshape(128, 128, 128), ("row", "col"), split_axis=0, concat_axis=0, tiled=True
    )
    lower, inverse = factor(pos, corner_lo, corner_hi)
    main, lower, lo, hi = lax.optimization_barrier((main, lower, lo, hi))
    lo, hi = ring(lo, "x"), ring(hi, "z")
    front, own_left = assemble(pos, marks, pattern, diag, main.reshape(16384, 128))
    lefts = own_front(own_left, my_core)
    w = left(pos, lefts, inverse, lower)
    kept = w[:, :1280]
    given = jnp.concatenate([w[:, :1024], w[:, 1280:]], axis=1)
    w = jnp.stack([kept, lax.ppermute(given, "col", CORE)])
    result = schur(pos, front, w, lo, hi)
    return result.reshape(2, 1, 1, 256, 8, 1, 256)


def solution(mesh):
    in_specs = (P(None, "row", "col"), P(None, "row"), P(None, None, "row", None), P())
    out_specs = P(None, None, "row", None, None, "col", None)
    return jax.shard_map(shards, mesh=mesh, in_specs=in_specs, out_specs=out_specs, check_vma=False)
```

```python
import jax
import jax.numpy as jnp
from jax import lax
from jax.experimental import pallas as pl
from jax.experimental.pallas import tpu as pltpu
from jax.sharding import PartitionSpec as P

F = 8192
P_SIZE = 1024
BS = 256
HI = lax.Precision.HIGHEST
VM = pl.BlockSpec(memory_space=pltpu.VMEM)
SM = pl.BlockSpec(memory_space=pltpu.SMEM)
F32 = jnp.float32


def params():
    return pltpu.CompilerParams(vmem_limit_bytes=60 * 1024 * 1024)


def dot_nn(a, b):
    return lax.dot_general(a, b, (((1,), (0,)), ((), ())), precision=HI, preferred_element_type=F32)


def dot_nt(a, b):
    return lax.dot_general(a, b, (((1,), (1,)), ((), ())), precision=HI, preferred_element_type=F32)


def dot_tn(a, b):
    return lax.dot_general(a, b, (((0,), (0,)), ((), ())), precision=HI, preferred_element_type=F32)


def head_kernel(pos_ref, t_ref, x_ref, diag_ref, panel_ref, marks_ref, slots_ref, cnt):
    my_col = pos_ref[1]

    def clear(i, _):
        cnt[i] = 0
        for k in range(16):
            marks_ref[i // 2, (i % 2) * 16 + k] = 256
        return 0

    lax.fori_loop(0, 64, clear, 0)
    for i in range(32):
        panel_ref[pl.ds(i * 72 + 64, 2), :] = diag_ref[i // 16]

    def place_rows(group, _):
        first = pl.multiple_of(group * 8, 8)
        for f in range(2):
            for k in range(8):
                target = t_ref[f, first + k]
                owner = lax.shift_right_logical(target, 8)
                slot = cnt[f * 32 + owner]
                cnt[f * 32 + owner] = slot + 1
                marks_ref[owner, f * 16 + slot] = jnp.bitwise_and(target, 255)
                slots_ref[f, first + k] = owner * 128 + slot

                @pl.when(owner < 4)
                def _():
                    for j in range(16):
                        u, c, h = j // 8, (j // 2) % 4, j % 2
                        q = jnp.bitwise_and(c + 4 - my_col, 3)
                        dest = f * 16 + u * 8 + q * 2 + h
                        panel_ref[pl.ds(dest * 72 + owner * 16 + slot, 1), :] = (
                            x_ref[f, pl.ds(first, 8), j * 128:(j + 1) * 128][k:k + 1, :]
                        )

        return 0

    lax.fori_loop(0, 32, place_rows, 0)


def build_head(pos, targets, contrib, diag):
    return pl.pallas_call(
        head_kernel,
        out_shape=(
            jax.ShapeDtypeStruct((32 * 72, 128), F32),
            jax.ShapeDtypeStruct((32, 32), jnp.int32),
            jax.ShapeDtypeStruct((2, 256), jnp.int32),
        ),
        in_specs=[SM, SM, VM, VM],
        out_specs=(VM, SM, SM),
        scratch_shapes=[pltpu.SMEM((64,), jnp.int32)],
        compiler_params=params(),
    )(pos, targets, contrib, diag)


def main_kernel(slots_ref, x_ref, main_ref, buf):
    for f in range(2):
        for j in range(16):
            block, half = j // 2, j % 2
            place = (block % 4) * 4 + (block // 4) * 2 + half
            buf[pl.ds(f * 4096 + place, 256, stride=16), :] = x_ref[f, :, j * 128:(j + 1) * 128]

    def place_row(i, _):
        for f in range(2):
            at = slots_ref[f, i]
            source = (f * 256 + i) * 16
            for c in range(4):
                main_ref[pl.ds((at + (c * 2 + f) * 16) * 4, 4), :] = buf[pl.ds(source + c * 4, 4), :]
        return 0

    lax.fori_loop(0, 256, place_row, 0, unroll=2)


def build_main(slots, contrib):
    return pl.pallas_call(
        main_kernel,
        out_shape=jax.ShapeDtypeStruct((16384, 128), F32),
        in_specs=[SM, VM],
        out_specs=VM,
        scratch_shapes=[pltpu.VMEM((8192, 128), F32)],
        compiler_params=params(),
        cost_estimate=pl.CostEstimate(flops=10**10, bytes_accessed=2**23, transcendentals=0),
    )(slots, contrib)


def eye128():
    return (
        lax.broadcasted_iota(jnp.int32, (128, 128), 0) == lax.broadcasted_iota(jnp.int32, (128, 128), 1)
    ).astype(F32)


def panel_kernel(pos_ref, marks_ref, pattern_ref, x_ref, out_ref, acc):
    my_row, my_col = pos_ref[0], pos_ref[1]
    f, u, q, h = my_row // 16, (my_row // 8) % 2, (my_row // 2) % 4, my_row % 2
    block = 8 * my_col + u * 4 + (q + my_col) % 4
    acc[...] = jnp.zeros_like(acc)

    def source(s, _):
        def step(k, _):
            rows = [n * 264 + marks_ref[s, 32 + n * 16 + k] for n in range(4)]
            new = [
                acc[pl.ds(rows[n], 1), :] + x_ref[pl.ds(s * 72 + n * 16 + k, 1), :] for n in range(4)
            ]
            for n in range(4):
                acc[pl.ds(rows[n], 1), :] = new[n]
            return 0

        return lax.fori_loop(0, 16, step, 0, unroll=4)

    lax.fori_loop(0, 32, source, 0)
    scale = jnp.where(block >= 4, pattern_ref[f, block], 1).astype(F32)
    for n in range(4):
        out_ref[pl.ds(n * 256, 256), :] = acc[n * 264:n * 264 + 256, :] * scale

    @pl.when(block < 4)
    def _():
        start = pl.multiple_of(block * 256 + h * 128, 128)
        shift = x_ref[pl.ds(block * 72 + 64 + h, 1), :]
        out_ref[pl.ds(start, 128), :] += eye128() * shift


def panel_piece(pos, marks, pattern, received):
    return pl.pallas_call(
        panel_kernel,
        out_shape=jax.ShapeDtypeStruct((1024, 128), F32),
        in_specs=[SM, SM, SM, VM],
        out_specs=VM,
        scratch_shapes=[pltpu.VMEM((1056, 128), F32)],
        compiler_params=params(),
    )(pos, marks, pattern, received)


SRCS = 8


def assemble_kernel(pos_ref, marks_ref, pattern_ref, diag_ref, x_ref, out_ref, left_ref, acc):
    step = pl.program_id(0)
    my_row, my_col = pos_ref[0], pos_ref[1]

    @pl.when(step == 0)
    def _():
        acc[...] = jnp.zeros_like(acc)

    def source(s, _):
        def slot(k, _):
            at = [marks_ref[step * SRCS + s, f * 16 + k] * 16 for f in range(2)]
            new = [
                acc[f, pl.ds(at[f] + c * 4, 4), :]
                + x_ref[pl.ds((((s * 4 + c) * 2 + f) * 16 + k) * 4, 4), :]
                for f in range(2) for c in range(4)
            ]
            for f in range(2):
                for c in range(4):
                    acc[f, pl.ds(at[f] + c * 4, 4), :] = new[f * 4 + c]
            return 0

        return lax.fori_loop(0, 16, slot, 0)

    lax.fori_loop(0, SRCS, source, 0)

    @pl.when(step == pl.num_programs(0) - 1)
    def _():
        for f in range(2):
            scale = jnp.where(my_row >= 4, pattern_ref[f, my_row], 1).astype(F32)

            @pl.when(my_row % 4 == my_col)
            def _():
                for h in range(2):
                    at = pl.ds(h * 2048 + (my_row // 4) * 2 + h, 128, stride=16)
                    acc[f, at, :] += eye128() * diag_ref[f, h:h + 1, :]

            for h in range(2):
                left_ref[f, :, h * 128:(h + 1) * 128] = acc[f, pl.ds(h, 256, stride=16), :] * scale
            out_ref[f] = acc[f, :4096, :]


def assemble(pos, marks, pattern, diag, received):
    chunk = SRCS * 512
    return pl.pallas_call(
        assemble_kernel,
        grid=(32 // SRCS,),
        out_shape=(
            jax.ShapeDtypeStruct((2, 4096, 128), F32),
            jax.ShapeDtypeStruct((2, 256, 256), F32),
        ),
        in_specs=[SM, SM, SM, VM, pl.BlockSpec((chunk, 128), lambda s: (s, 0))],
        out_specs=(
            pl.BlockSpec((2, 4096, 128), lambda s: (0, 0, 0)),
            pl.BlockSpec((2, 256, 256), lambda s: (0, 0, 0)),
        ),
        scratch_shapes=[pltpu.VMEM((2, 4112, 128), F32)],
        compiler_params=params(),
        cost_estimate=pl.CostEstimate(flops=10**6, bytes_accessed=2**12, transcendentals=0),
    )(pos, marks, pattern, diag, received)


def factor_steps(steps, l_ref, x_ref, d_ref):
    lanes = lax.broadcasted_iota(jnp.int32, (8, 128), 1)
    subs = lax.broadcasted_iota(jnp.int32, (8, 128), 0)
    low = lax.broadcasted_iota(jnp.int32, (128, 128), 0) >= lax.broadcasted_iota(jnp.int32, (128, 128), 1)

    for p in steps:
        here = slice(p * 128, (p + 1) * 128)
        d_ref[:, :128] = l_ref[here, here]
        d_ref[:, 128:] = eye128()

        def group(g, _):
            rows = d_ref[pl.ds(pl.multiple_of(g * 8, 8), 8), :]
            a8, r8 = rows[:, :128], rows[:, 128:]
            turned = pltpu.roll(a8, (128 - g * 8) % 128, 1)
            cols = [jnp.broadcast_to(turned[:, j:j + 1], (8, 128)) for j in range(8)]
            for j in range(8):
                pivot = jnp.broadcast_to(cols[j][j:j + 1, :], (8, 128))
                root = lax.rsqrt(pivot)
                root = root * (1.5 - 0.5 * pivot * root * root)
                mult = jnp.where(subs > j, cols[j] * root, 0.0)
                for k in range(j + 1, 8):
                    cols[k] = cols[k] - mult * (cols[k][j:j + 1, :] * root)
                ua, ur = a8[j:j + 1, :] * root, r8[j:j + 1, :] * root
                a8 = jnp.where(subs == j, ua, a8 - mult * ua)
                r8 = jnp.where(subs == j, ur, r8 - mult * ur)
            new = jnp.concatenate([a8, r8], axis=1)
            d_ref[pl.ds(pl.multiple_of(g * 8, 8), 8), :] = new
            later = jnp.where(lanes > g * 8 + 7, a8, 0.0)
            d_ref[...] = d_ref[...] - dot_tn(later, new)
            return 0

        lax.fori_loop(0, 16, group, 0)
        inverse = jnp.where(low, d_ref[:, 128:], 0.0)
        l_ref[here, here] = jnp.where(low, d_ref[:, :128].T, 0.0)
        x_ref[here, here] = inverse
        if p > 0:
            done = p * 128
            both = dot_nn(l_ref[here, :done], x_ref[:done, :done])
            x_ref[here, :done] = -dot_nn(inverse, both)
        if p < 7:
            after = (p + 1) * 128
            l_ref[here, after:] = jnp.zeros((128, 1024 - after), F32)
            x_ref[here, after:] = jnp.zeros((128, 1024 - after), F32)
            l_ref[after:, here] = dot_nt(l_ref[after:, here], inverse)
            for i in range(p + 1, 8):
                mine = slice(i * 128, (i + 1) * 128)
                upto = slice(after, (i + 1) * 128)
                l_ref[mine, upto] = l_ref[mine, upto] - dot_nt(l_ref[mine, here], l_ref[upto, here])


def factor_kernel(pos_ref, lo_ref, hi_ref, l_ref, x_ref, d_ref):
    my_z = (pos_ref[0] // 2) % 4

    def corner(rows, block):
        ref = lo_ref if rows < 4 else hi_ref
        return ref[(my_z + 4 - block // 2) % 4, block % 2, (rows % 4) * 128:(rows % 4 + 1) * 128, :]

    for i in range(8):
        for j in range(i + 1):
            l_ref[i * 128:(i + 1) * 128, j * 128:(j + 1) * 128] = 0.5 * (corner(i, j) + corner(j, i).T)
    factor_steps(range(8), l_ref, x_ref, d_ref)


def factor(pos, corner_lo, corner_hi):
    whole = jax.ShapeDtypeStruct((1024, 1024), F32)
    return pl.pallas_call(
        factor_kernel,
        out_shape=(whole, whole),
        in_specs=[SM, VM, VM],
        out_specs=(VM, VM),
        scratch_shapes=[pltpu.VMEM((128, 256), F32)],
        compiler_params=params(),
        cost_estimate=pl.CostEstimate(flops=10**11, bytes_accessed=12 * 2**20, transcendentals=0),
    )(pos, corner_lo, corner_hi)


def left_kernel(pos_ref, a_ref, x_ref, head_ref, w_ref, wide, rows):
    my_row, my_col = pos_ref[0], pos_ref[1]
    for far in range(2):
        for core in range(2):
            column = jnp.bitwise_xor(my_col, core + 2 * far)
            wide[:, pl.ds(pl.multiple_of(column * 256, 256), 256)] = a_ref[far, core]
    for b in range(4):
        here = slice(b * 256, (b + 1) * 256)
        rows[:, here] = dot_nt(wide[:, :(b + 1) * 256], x_ref[here, :(b + 1) * 256])
    for b in range(4):
        here = slice(b * 256, (b + 1) * 256)
        w_ref[:, here] = dot_nn(rows[:, b * 256:], x_ref[b * 256:, here])

    @pl.when(my_row < 4)
    def _():
        rows[...] = head_ref[...]

    for core in range(2):
        column = pl.multiple_of(jnp.bitwise_xor(my_col, core) * 256, 256)
        w_ref[:, 1024 + core * 256:1280 + core * 256] = rows[:, pl.ds(column, 256)]


def left(pos, a, inverse, lower):
    return pl.pallas_call(
        left_kernel,
        grid_spec=pltpu.PrefetchScalarGridSpec(
            num_scalar_prefetch=1,
            grid=(1,),
            in_specs=[
                pl.BlockSpec((2, 2, 256, 256), lambda i, pos: (0, 0, 0, 0)),
                pl.BlockSpec((1024, 1024), lambda i, pos: (0, 0)),
                pl.BlockSpec((256, 1024), lambda i, pos: (jnp.minimum(pos[0], 3), 0)),
            ],
            out_specs=pl.BlockSpec((256, 1536), lambda i, pos: (0, 0)),
            scratch_shapes=[pltpu.VMEM((256, 1024), F32), pltpu.VMEM((256, 1024), F32)],
        ),
        out_shape=jax.ShapeDtypeStruct((256, 1536), F32),
        compiler_params=params(),
        cost_estimate=pl.CostEstimate(flops=10**6, bytes_accessed=2**12, transcendentals=0),
    )(pos, a, inverse, lower)


def schur_kernel(pos_ref, front_ref, w_ref, *refs):
    out_ref, partial = refs[10], refs[11]
    f, j = pl.program_id(0), pl.program_id(1)
    my_row = pos_ref[0]
    par = my_row % 2
    block = 2 * (j % 4) + j // 4
    x, z = f * 2 + j // 4, (pos_ref[1] + 4 - j % 4) % 4
    turned = ((my_row // 8 + 4 - x) % 4, ((my_row // 2) % 4 + 4 - z) % 4)
    places = [pl.ds(2 * block + h, 256, stride=16) for h in range(2)]

    def columns(ref, rows):
        return jnp.concatenate([ref[0, jnp.bitwise_xor(par, h), rows, :] for h in range(2)], axis=1)

    def put(value):
        for h in range(2):
            out_ref[0, places[h], :] = value[:, h * 128:(h + 1) * 128]

    @pl.when(j == 0)
    def _():
        put(w_ref[0, :, 1024:1280])

    for part in range(2):
        own, below, first, second, above = refs[5 * part:5 * part + 5]
        for k, sources in enumerate(((own,), (below,), (first, second), (above,))):
            here = (j > 0) & (turned[part] == k)
            rows = 512 // len(sources)

            @pl.when(here & (my_row >= 4))
            def _():
                total = 0.0
                for i, ref in enumerate(sources):
                    start = part * 512 + i * rows
                    total += dot_nn(w_ref[0, :, start:start + rows], columns(ref, slice(0, rows)))
                if part == 0:
                    partial[...] = total
                else:
                    total = total + partial[...]
                    for h in range(2):
                        out_ref[0, places[h], :] = (
                            front_ref[0, places[h], :] - total[:, h * 128:(h + 1) * 128]
                        )

            for i in range(2):

                @pl.when(here & (my_row == part * 2 + i))
                def _():
                    if len(sources) == 2:
                        put(columns(sources[i], slice(0, 256)))
                    else:
                        put(columns(sources[0], slice(i * 256, (i + 1) * 256)))


def schur(pos, front, w, lo, hi):
    def z_rel(j, pos):
        return ((pos[0] // 2) % 4 + 4 - (pos[1] + 4 - j % 4) % 4) % 4

    def lo_map(k):
        def index(f, j, pos):
            x, mine = f * 2 + j // 4, (pos[0] // 8 + 4 - k) % 4
            idle = jnp.where(x < mine, z_rel(0, pos), z_rel(3, pos))
            return jnp.where(x == mine, z_rel(j, pos), idle), 0, 0, 0

        return index

    def hi_map(f, j, pos):
        return (pos[0] // 8 + 4 - (f * 2 + j // 4)) % 4, 0, 0, 0

    def fixed(f, j, pos):
        return f, 0, 0

    rows = (512, 512, 256, 256, 512)
    return pl.pallas_call(
        schur_kernel,
        grid_spec=pltpu.PrefetchScalarGridSpec(
            num_scalar_prefetch=1,
            grid=(2, 8),
            in_specs=[
                pl.BlockSpec((1, 4096, 128), fixed),
                pl.BlockSpec(
                    (1, 256, 1280), lambda f, j, pos: (jnp.bitwise_xor(f, pos[1] % 2), 0, 0)
                ),
            ]
            + [pl.BlockSpec((1, 2, n, 128), lo_map(k)) for n, k in zip(rows, (0, 1, 2, 2, 3))]
            + [pl.BlockSpec((1, 2, n, 128), hi_map) for n in rows],
            out_specs=pl.BlockSpec((1, 4096, 128), fixed),
            scratch_shapes=[pltpu.VMEM((256, 256), F32)],
        ),
        out_shape=jax.ShapeDtypeStruct((2, 4096, 128), F32),
        compiler_params=params(),
    )(pos, front, w, *lo, *hi)


def turn(axis, by):
    pairs = []
    for x in range(4):
        for z in range(4):
            for y in range(2):
                to = ((x + by) % 4, z) if axis == "x" else (x, (z + by) % 4)
                pairs.append((x * 8 + z * 2 + y, to[0] * 8 + to[1] * 2 + y))
    return pairs


def ring(value, axis):
    forth, back = turn(axis, 1), turn(axis, -1)
    half = value.shape[-2] // 2
    below = lax.ppermute(value, "row", forth)
    above = lax.ppermute(value, "row", back)
    first = lax.ppermute(below[..., :half, :], "row", forth)
    second = lax.ppermute(above[..., half:, :], "row", back)
    return value, below, first, second, above


def short_ring(value, axis, opposite=None):
    if opposite is None:
        opposite = lax.ppermute(value, "row", turn(axis, 2))
    below, above = (lax.ppermute(value, "row", turn(axis, by)) for by in (1, -1))
    return jnp.stack([value, below, opposite, above])


def across(value, pairs, axis):
    return jnp.stack([value, lax.ppermute(value, axis, pairs)])


CORE = [(0, 1), (1, 0), (2, 3), (3, 2)]
FAR = [(0, 2), (2, 0), (1, 3), (3, 1)]
NEAR = [(i, i ^ 1) for i in range(32)]


def own_front(value, my_core):
    kept = lax.dynamic_index_in_dim(value, my_core, 0, keepdims=False)
    given = lax.dynamic_index_in_dim(value, 1 - my_core, 0, keepdims=False)
    return across(jnp.stack([kept, lax.ppermute(given, "col", CORE)]), FAR, "col")


def device(x, z, y, core):
    return (x * 8 + z * 2 + y % 2) * 4 + (y // 2) * 2 + core


def corner_columns(piece, my_x, my_z, my_y, my_core):
    both = ("row", "col")
    got = []
    for k in range(4):
        pairs = [
            (device(2 * f, z, h, 0), device(2 * f, z, (h + k) % 4, f))
            for f in range(2) for z in range(4) for h in range(2)
        ]
        got.append(lax.ppermute(piece, both, pairs))
    got = jnp.stack(got)
    pair = jnp.stack(
        [lax.dynamic_index_in_dim(got, (my_y + 4 - h) % 4, 0, keepdims=False) for h in range(2)]
    )
    away = (my_x + 4 - 2 * my_core) % 4

    def spread_x(value):
        half = value.shape[-2] // 2

        def moved(part, start, by):
            pairs = [
                (device((2 * core + start) % 4, z, y, core), device((2 * core + start + by) % 4, z, y, core))
                for z in range(4) for y in range(4) for core in range(2)
            ]
            return lax.ppermute(part, both, pairs)

        below, above = moved(value, 0, 1), moved(value, 0, -1)
        if value.ndim == 3:
            far = moved(value, 0, 2)
        else:
            far = jnp.concatenate(
                [moved(below[..., :half, :], 1, 1), moved(above[..., half:, :], 3, -1)], axis=-2
            )
        return jnp.where(away == 0, value, jnp.where(away == 1, below, jnp.where(away == 3, above, far)))

    def ring_z(value, xs):
        def moved(part, by):
            pairs = [
                (device(x, z, y, core), device(x, (z + by) % 4, y, core))
                for z in range(4) for y in range(4) for core in range(2) for x in xs(core)
            ]
            return lax.ppermute(part, both, pairs)

        return jnp.stack([value] + [moved(value, by) for by in (1, 2, -1)])

    lo = spread_x(ring_z(pair[:, :512], lambda core: [2 * core]))
    hi = ring_z(spread_x(pair[:, 512:]), lambda core: range(4))
    return lo, hi


def shards(contrib, target_rows, diag_shift, pattern):
    my_row = lax.axis_index("row").astype(jnp.int32)
    my_col = lax.axis_index("col").astype(jnp.int32)
    my_core = my_col % 2
    my_x, my_z, my_y = my_row // 8, (my_row // 2) % 4, (my_col // 2) * 2 + my_row % 2
    pos = jnp.stack([my_row, my_col])
    diag = diag_shift.reshape(2, 2, 128)
    panel, marks, slots = build_head(pos, target_rows, contrib, diag)
    heads = jnp.swapaxes(marks[:4].reshape(4, 2, 16), 0, 1).reshape(2, 1, 64)
    heads = jnp.broadcast_to(heads, (2, 16, 64)).reshape(32, 64)
    marks = jnp.concatenate([marks, heads, heads[:, :32]], axis=1).astype(F32)
    panel = panel.reshape(32, 72, 128).at[:, 66, :].set(marks)
    panel = lax.all_to_all(panel, "row", split_axis=0, concat_axis=0, tiled=True)
    marks = panel[:, 66, :96].astype(jnp.int32)
    piece = panel_piece(pos, marks, pattern, panel.reshape(32 * 72, 128))
    slots, piece = lax.optimization_barrier((slots, piece))
    main = build_main(slots, contrib)
    corner_lo, corner_hi = corner_columns(piece, my_x, my_z, my_y, my_core)
    moves = [
        (i * 4 + c, i * 4 + ((i // 2) % 4 + c) % 4) for i in range(32) for c in range(4)
    ]
    pair = across(lax.ppermute(piece, ("row", "col"), moves), NEAR, "row")
    opposite = lax.ppermute(pair[:, :512], "row", turn("z", 2))
    corner_lo, corner_hi, main, pair, opposite = lax.optimization_barrier(
        (corner_lo, corner_hi, main, pair, opposite)
    )
    lo, hi = short_ring(pair[:, :512], "z", opposite), short_ring(pair[:, 512:], "x")
    main = lax.all_to_all(
        main.reshape(128, 128, 128), ("row", "col"), split_axis=0, concat_axis=0, tiled=True
    )
    lower, inverse = factor(pos, corner_lo, corner_hi)
    main, lower, lo, hi = lax.optimization_barrier((main, lower, lo, hi))
    lo, hi = ring(lo, "x"), ring(hi, "z")
    front, own_left = assemble(pos, marks, pattern, diag, main.reshape(16384, 128))
    lefts = own_front(own_left, my_core)
    w = left(pos, lefts, inverse, lower)
    kept = w[:, :1280]
    given = jnp.concatenate([w[:, :1024], w[:, 1280:]], axis=1)
    w = jnp.stack([kept, lax.ppermute(given, "col", CORE)])
    result = schur(pos, front, w, lo, hi)
    return result.reshape(2, 1, 1, 256, 8, 1, 256)


def solution(mesh):
    in_specs = (P(None, "row", "col"), P(None, "row"), P(None, None, "row", None), P())
    out_specs = P(None, None, "row", None, None, "col", None)
    return jax.shard_map(shards, mesh=mesh, in_specs=in_specs, out_specs=out_specs, check_vma=False)
```

```python
import jax
import jax.numpy as jnp
from jax import lax
from jax.experimental import pallas as pl
from jax.experimental.pallas import tpu as pltpu
from jax.sharding import PartitionSpec as P

F = 8192
P_SIZE = 1024
BS = 256
HI = lax.Precision.HIGHEST
VM = pl.BlockSpec(memory_space=pltpu.VMEM)
SM = pl.BlockSpec(memory_space=pltpu.SMEM)
F32 = jnp.float32


def params():
    return pltpu.CompilerParams(vmem_limit_bytes=60 * 1024 * 1024)


def dot_nn(a, b):
    return lax.dot_general(a, b, (((1,), (0,)), ((), ())), precision=HI, preferred_element_type=F32)


def dot_nt(a, b):
    return lax.dot_general(a, b, (((1,), (1,)), ((), ())), precision=HI, preferred_element_type=F32)


def dot_tn(a, b):
    return lax.dot_general(a, b, (((0,), (0,)), ((), ())), precision=HI, preferred_element_type=F32)


def head_kernel(pos_ref, t_ref, x_ref, diag_ref, panel_ref, marks_ref, slots_ref, cnt):
    my_col = pos_ref[1]

    def clear(i, _):
        cnt[i] = 0
        for k in range(16):
            marks_ref[i // 2, (i % 2) * 16 + k] = 256
        return 0

    lax.fori_loop(0, 64, clear, 0)
    for i in range(32):
        panel_ref[pl.ds(i * 72 + 64, 2), :] = diag_ref[i // 16]

    def place_rows(group, _):
        first = pl.multiple_of(group * 8, 8)
        for f in range(2):
            for k in range(8):
                target = t_ref[f, first + k]
                owner = lax.shift_right_logical(target, 8)
                slot = cnt[f * 32 + owner]
                cnt[f * 32 + owner] = slot + 1
                marks_ref[owner, f * 16 + slot] = jnp.bitwise_and(target, 255)
                slots_ref[f, first + k] = owner * 128 + slot

                @pl.when(owner < 4)
                def _():
                    for j in range(16):
                        u, c, h = j // 8, (j // 2) % 4, j % 2
                        q = jnp.bitwise_and(c + 4 - my_col, 3)
                        dest = f * 16 + u * 8 + q * 2 + h
                        panel_ref[pl.ds(dest * 72 + owner * 16 + slot, 1), :] = (
                            x_ref[f, pl.ds(first, 8), j * 128:(j + 1) * 128][k:k + 1, :]
                        )

        return 0

    lax.fori_loop(0, 32, place_rows, 0)


def build_head(pos, targets, contrib, diag):
    return pl.pallas_call(
        head_kernel,
        out_shape=(
            jax.ShapeDtypeStruct((32 * 72, 128), F32),
            jax.ShapeDtypeStruct((32, 32), jnp.int32),
            jax.ShapeDtypeStruct((2, 256), jnp.int32),
        ),
        in_specs=[SM, SM, VM, VM],
        out_specs=(VM, SM, SM),
        scratch_shapes=[pltpu.SMEM((64,), jnp.int32)],
        compiler_params=params(),
    )(pos, targets, contrib, diag)


def main_kernel(slots_ref, x_ref, main_ref, buf):
    for f in range(2):
        for j in range(16):
            block, half = j // 2, j % 2
            place = (block % 4) * 4 + (block // 4) * 2 + half
            buf[pl.ds(f * 4096 + place, 256, stride=16), :] = x_ref[f, :, j * 128:(j + 1) * 128]

    def place_row(i, _):
        for f in range(2):
            at = slots_ref[f, i]
            source = (f * 256 + i) * 16
            for c in range(4):
                main_ref[pl.ds((at + (c * 2 + f) * 16) * 4, 4), :] = buf[pl.ds(source + c * 4, 4), :]
        return 0

    lax.fori_loop(0, 256, place_row, 0, unroll=2)


def build_main(slots, contrib):
    return pl.pallas_call(
        main_kernel,
        out_shape=jax.ShapeDtypeStruct((16384, 128), F32),
        in_specs=[SM, VM],
        out_specs=VM,
        scratch_shapes=[pltpu.VMEM((8192, 128), F32)],
        compiler_params=params(),
        cost_estimate=pl.CostEstimate(flops=10**10, bytes_accessed=2**23, transcendentals=0),
    )(slots, contrib)


def eye128():
    return (
        lax.broadcasted_iota(jnp.int32, (128, 128), 0) == lax.broadcasted_iota(jnp.int32, (128, 128), 1)
    ).astype(F32)


def panel_kernel(pos_ref, marks_ref, pattern_ref, x_ref, out_ref, acc):
    my_row, my_col = pos_ref[0], pos_ref[1]
    f, u, q, h = my_row // 16, (my_row // 8) % 2, (my_row // 2) % 4, my_row % 2
    block = 8 * my_col + u * 4 + (q + my_col) % 4
    acc[...] = jnp.zeros_like(acc)

    def source(s, _):
        def step(k, _):
            rows = [n * 264 + marks_ref[s, 32 + n * 16 + k] for n in range(4)]
            new = [
                acc[pl.ds(rows[n], 1), :] + x_ref[pl.ds(s * 72 + n * 16 + k, 1), :] for n in range(4)
            ]
            for n in range(4):
                acc[pl.ds(rows[n], 1), :] = new[n]
            return 0

        return lax.fori_loop(0, 16, step, 0, unroll=4)

    lax.fori_loop(0, 32, source, 0)
    scale = jnp.where(block >= 4, pattern_ref[f, block], 1).astype(F32)
    for n in range(4):
        out_ref[pl.ds(n * 256, 256), :] = acc[n * 264:n * 264 + 256, :] * scale

    @pl.when(block < 4)
    def _():
        start = pl.multiple_of(block * 256 + h * 128, 128)
        shift = x_ref[pl.ds(block * 72 + 64 + h, 1), :]
        out_ref[pl.ds(start, 128), :] += eye128() * shift


def panel_piece(pos, marks, pattern, received):
    return pl.pallas_call(
        panel_kernel,
        out_shape=jax.ShapeDtypeStruct((1024, 128), F32),
        in_specs=[SM, SM, SM, VM],
        out_specs=VM,
        scratch_shapes=[pltpu.VMEM((1056, 128), F32)],
        compiler_params=params(),
    )(pos, marks, pattern, received)


SRCS = 8


def assemble_kernel(pos_ref, marks_ref, pattern_ref, diag_ref, x_ref, out_ref, left_ref, acc):
    step = pl.program_id(0)
    my_row, my_col = pos_ref[0], pos_ref[1]

    @pl.when(step == 0)
    def _():
        acc[...] = jnp.zeros_like(acc)

    def source(s, _):
        def slot(k, _):
            at = [marks_ref[step * SRCS + s, f * 16 + k] * 16 for f in range(2)]
            new = [
                acc[f, pl.ds(at[f] + c * 4, 4), :]
                + x_ref[pl.ds((((s * 4 + c) * 2 + f) * 16 + k) * 4, 4), :]
                for f in range(2) for c in range(4)
            ]
            for f in range(2):
                for c in range(4):
                    acc[f, pl.ds(at[f] + c * 4, 4), :] = new[f * 4 + c]
            return 0

        return lax.fori_loop(0, 16, slot, 0)

    lax.fori_loop(0, SRCS, source, 0)

    @pl.when(step == pl.num_programs(0) - 1)
    def _():
        for f in range(2):
            scale = jnp.where(my_row >= 4, pattern_ref[f, my_row], 1).astype(F32)

            @pl.when(my_row % 4 == my_col)
            def _():
                for h in range(2):
                    at = pl.ds(h * 2048 + (my_row // 4) * 2 + h, 128, stride=16)
                    acc[f, at, :] += eye128() * diag_ref[f, h:h + 1, :]

            for h in range(2):
                left_ref[f, :, h * 128:(h + 1) * 128] = acc[f, pl.ds(h, 256, stride=16), :] * scale
            out_ref[f] = acc[f, :4096, :]


def assemble(pos, marks, pattern, diag, received):
    chunk = SRCS * 512
    return pl.pallas_call(
        assemble_kernel,
        grid=(32 // SRCS,),
        out_shape=(
            jax.ShapeDtypeStruct((2, 4096, 128), F32),
            jax.ShapeDtypeStruct((2, 256, 256), F32),
        ),
        in_specs=[SM, SM, SM, VM, pl.BlockSpec((chunk, 128), lambda s: (s, 0))],
        out_specs=(
            pl.BlockSpec((2, 4096, 128), lambda s: (0, 0, 0)),
            pl.BlockSpec((2, 256, 256), lambda s: (0, 0, 0)),
        ),
        scratch_shapes=[pltpu.VMEM((2, 4112, 128), F32)],
        compiler_params=params(),
        cost_estimate=pl.CostEstimate(flops=10**6, bytes_accessed=2**12, transcendentals=0),
    )(pos, marks, pattern, diag, received)


def factor_steps(steps, l_ref, x_ref, d_ref):
    lanes = lax.broadcasted_iota(jnp.int32, (8, 128), 1)
    subs = lax.broadcasted_iota(jnp.int32, (8, 128), 0)
    low = lax.broadcasted_iota(jnp.int32, (128, 128), 0) >= lax.broadcasted_iota(jnp.int32, (128, 128), 1)

    for p in steps:
        here = slice(p * 128, (p + 1) * 128)
        d_ref[:, :128] = l_ref[here, here]
        d_ref[:, 128:] = eye128()

        def group(g, _):
            rows = d_ref[pl.ds(pl.multiple_of(g * 8, 8), 8), :]
            a8, r8 = rows[:, :128], rows[:, 128:]
            turned = pltpu.roll(a8, (128 - g * 8) % 128, 1)
            cols = [jnp.broadcast_to(turned[:, j:j + 1], (8, 128)) for j in range(8)]
            for j in range(8):
                pivot = jnp.broadcast_to(cols[j][j:j + 1, :], (8, 128))
                root = lax.rsqrt(pivot)
                root = root * (1.5 - 0.5 * pivot * root * root)
                mult = jnp.where(subs > j, cols[j] * root, 0.0)
                for k in range(j + 1, 8):
                    cols[k] = cols[k] - mult * (cols[k][j:j + 1, :] * root)
                ua, ur = a8[j:j + 1, :] * root, r8[j:j + 1, :] * root
                a8 = jnp.where(subs == j, ua, a8 - mult * ua)
                r8 = jnp.where(subs == j, ur, r8 - mult * ur)
            new = jnp.concatenate([a8, r8], axis=1)
            d_ref[pl.ds(pl.multiple_of(g * 8, 8), 8), :] = new
            later = jnp.where(lanes > g * 8 + 7, a8, 0.0)
            d_ref[...] = d_ref[...] - dot_tn(later, new)
            return 0

        lax.fori_loop(0, 16, group, 0)
        inverse = jnp.where(low, d_ref[:, 128:], 0.0)
        l_ref[here, here] = jnp.where(low, d_ref[:, :128].T, 0.0)
        x_ref[here, here] = inverse
        if p > 0:
            done = p * 128
            both = dot_nn(l_ref[here, :done], x_ref[:done, :done])
            x_ref[here, :done] = -dot_nn(inverse, both)
        if p < 7:
            after = (p + 1) * 128
            l_ref[here, after:] = jnp.zeros((128, 1024 - after), F32)
            x_ref[here, after:] = jnp.zeros((128, 1024 - after), F32)
            l_ref[after:, here] = dot_nt(l_ref[after:, here], inverse)
            for i in range(p + 1, 8):
                mine = slice(i * 128, (i + 1) * 128)
                upto = slice(after, (i + 1) * 128)
                l_ref[mine, upto] = l_ref[mine, upto] - dot_nt(l_ref[mine, here], l_ref[upto, here])


def factor_kernel(pos_ref, lo_ref, hi_ref, l_ref, x_ref, d_ref):
    my_z = (pos_ref[0] // 2) % 4

    def corner(rows, block):
        ref = lo_ref if rows < 4 else hi_ref
        return ref[(my_z + 4 - block // 2) % 4, block % 2, (rows % 4) * 128:(rows % 4 + 1) * 128, :]

    for i in range(8):
        for j in range(i + 1):
            l_ref[i * 128:(i + 1) * 128, j * 128:(j + 1) * 128] = 0.5 * (corner(i, j) + corner(j, i).T)
    factor_steps(range(8), l_ref, x_ref, d_ref)


def factor(pos, corner_lo, corner_hi):
    whole = jax.ShapeDtypeStruct((1024, 1024), F32)
    return pl.pallas_call(
        factor_kernel,
        out_shape=(whole, whole),
        in_specs=[SM, VM, VM],
        out_specs=(VM, VM),
        scratch_shapes=[pltpu.VMEM((128, 256), F32)],
        compiler_params=params(),
        cost_estimate=pl.CostEstimate(flops=10**11, bytes_accessed=12 * 2**20, transcendentals=0),
    )(pos, corner_lo, corner_hi)


def left_kernel(pos_ref, a_ref, x_ref, head_ref, w_ref, wide, rows):
    my_row, my_col = pos_ref[0], pos_ref[1]
    for far in range(2):
        for core in range(2):
            column = jnp.bitwise_xor(my_col, core + 2 * far)
            wide[:, pl.ds(pl.multiple_of(column * 256, 256), 256)] = a_ref[far, core]
    for b in range(4):
        here = slice(b * 256, (b + 1) * 256)
        rows[:, here] = dot_nt(wide[:, :(b + 1) * 256], x_ref[here, :(b + 1) * 256])
    for b in range(4):
        here = slice(b * 256, (b + 1) * 256)
        w_ref[:, here] = dot_nn(rows[:, b * 256:], x_ref[b * 256:, here])

    @pl.when(my_row < 4)
    def _():
        rows[...] = head_ref[...]

    for core in range(2):
        column = pl.multiple_of(jnp.bitwise_xor(my_col, core) * 256, 256)
        w_ref[:, 1024 + core * 256:1280 + core * 256] = rows[:, pl.ds(column, 256)]


def left(pos, a, inverse, lower):
    return pl.pallas_call(
        left_kernel,
        grid_spec=pltpu.PrefetchScalarGridSpec(
            num_scalar_prefetch=1,
            grid=(1,),
            in_specs=[
                pl.BlockSpec((2, 2, 256, 256), lambda i, pos: (0, 0, 0, 0)),
                pl.BlockSpec((1024, 1024), lambda i, pos: (0, 0)),
                pl.BlockSpec((256, 1024), lambda i, pos: (jnp.minimum(pos[0], 3), 0)),
            ],
            out_specs=pl.BlockSpec((256, 1536), lambda i, pos: (0, 0)),
            scratch_shapes=[pltpu.VMEM((256, 1024), F32), pltpu.VMEM((256, 1024), F32)],
        ),
        out_shape=jax.ShapeDtypeStruct((256, 1536), F32),
        compiler_params=params(),
        cost_estimate=pl.CostEstimate(flops=10**6, bytes_accessed=2**12, transcendentals=0),
    )(pos, a, inverse, lower)


def split(value):
    high = value.astype(jnp.bfloat16)
    return high, (value - high.astype(F32)).astype(jnp.bfloat16)


def dot_16(a, b):
    return lax.dot_general(a, b, (((1,), (0,)), ((), ())), preferred_element_type=F32)


def schur_kernel(pos_ref, front_ref, w_ref, *refs):
    out_ref, partial, w_high, w_low = refs[10:]
    f, j = pl.program_id(0), pl.program_id(1)
    my_row = pos_ref[0]
    par = my_row % 2
    block = 2 * (j % 4) + j // 4
    x, z = f * 2 + j // 4, (pos_ref[1] + 4 - j % 4) % 4
    turned = ((my_row // 8 + 4 - x) % 4, ((my_row // 2) % 4 + 4 - z) % 4)
    places = [pl.ds(2 * block + h, 256, stride=16) for h in range(2)]

    def columns(ref, rows):
        return jnp.concatenate([ref[0, jnp.bitwise_xor(par, h), rows, :] for h in range(2)], axis=1)

    def put(value):
        for h in range(2):
            out_ref[0, places[h], :] = value[:, h * 128:(h + 1) * 128]

    @pl.when(j == 0)
    def _():
        put(w_ref[0, :, 1024:1280])
        w_high[...], w_low[...] = split(w_ref[0, :, :1024])

    for part in range(2):
        own, below, first, second, above = refs[5 * part:5 * part + 5]
        for k, sources in enumerate(((own,), (below,), (first, second), (above,))):
            here = (j > 0) & (turned[part] == k)
            rows = 512 // len(sources)

            @pl.when(here & (my_row >= 4))
            def _():
                total = 0.0
                for i, ref in enumerate(sources):
                    start = part * 512 + i * rows
                    high, low = split(columns(ref, slice(0, rows)))
                    own_high, own_low = w_high[:, start:start + rows], w_low[:, start:start + rows]
                    total += dot_16(own_high, low) + dot_16(own_low, high) + dot_16(own_high, high)
                if part == 0:
                    partial[...] = total
                else:
                    total = total + partial[...]
                    for h in range(2):
                        out_ref[0, places[h], :] = (
                            front_ref[0, places[h], :] - total[:, h * 128:(h + 1) * 128]
                        )

            for i in range(2):

                @pl.when(here & (my_row == part * 2 + i))
                def _():
                    if len(sources) == 2:
                        put(columns(sources[i], slice(0, 256)))
                    else:
                        put(columns(sources[0], slice(i * 256, (i + 1) * 256)))


def schur(pos, front, w, lo, hi):
    def z_rel(j, pos):
        return ((pos[0] // 2) % 4 + 4 - (pos[1] + 4 - j % 4) % 4) % 4

    def lo_map(k):
        def index(f, j, pos):
            x, mine = f * 2 + j // 4, (pos[0] // 8 + 4 - k) % 4
            idle = jnp.where(x < mine, z_rel(0, pos), z_rel(3, pos))
            return jnp.where(x == mine, z_rel(j, pos), idle), 0, 0, 0

        return index

    def hi_map(f, j, pos):
        return (pos[0] // 8 + 4 - (f * 2 + j // 4)) % 4, 0, 0, 0

    def fixed(f, j, pos):
        return f, 0, 0

    rows = (512, 512, 256, 256, 512)
    return pl.pallas_call(
        schur_kernel,
        grid_spec=pltpu.PrefetchScalarGridSpec(
            num_scalar_prefetch=1,
            grid=(2, 8),
            in_specs=[
                pl.BlockSpec((1, 4096, 128), fixed),
                pl.BlockSpec(
                    (1, 256, 1280), lambda f, j, pos: (jnp.bitwise_xor(f, pos[1] % 2), 0, 0)
                ),
            ]
            + [pl.BlockSpec((1, 2, n, 128), lo_map(k)) for n, k in zip(rows, (0, 1, 2, 2, 3))]
            + [pl.BlockSpec((1, 2, n, 128), hi_map) for n in rows],
            out_specs=pl.BlockSpec((1, 4096, 128), fixed),
            scratch_shapes=[
                pltpu.VMEM((256, 256), F32),
                pltpu.VMEM((256, 1024), jnp.bfloat16),
                pltpu.VMEM((256, 1024), jnp.bfloat16),
            ],
        ),
        out_shape=jax.ShapeDtypeStruct((2, 4096, 128), F32),
        compiler_params=params(),
    )(pos, front, w, *lo, *hi)


def turn(axis, by):
    pairs = []
    for x in range(4):
        for z in range(4):
            for y in range(2):
                to = ((x + by) % 4, z) if axis == "x" else (x, (z + by) % 4)
                pairs.append((x * 8 + z * 2 + y, to[0] * 8 + to[1] * 2 + y))
    return pairs


def ring(value, axis):
    forth, back = turn(axis, 1), turn(axis, -1)
    half = value.shape[-2] // 2
    below = lax.ppermute(value, "row", forth)
    above = lax.ppermute(value, "row", back)
    first = lax.ppermute(below[..., :half, :], "row", forth)
    second = lax.ppermute(above[..., half:, :], "row", back)
    return value, below, first, second, above


def short_ring(value, axis, opposite=None):
    if opposite is None:
        opposite = lax.ppermute(value, "row", turn(axis, 2))
    below, above = (lax.ppermute(value, "row", turn(axis, by)) for by in (1, -1))
    return jnp.stack([value, below, opposite, above])


def across(value, pairs, axis):
    return jnp.stack([value, lax.ppermute(value, axis, pairs)])


CORE = [(0, 1), (1, 0), (2, 3), (3, 2)]
FAR = [(0, 2), (2, 0), (1, 3), (3, 1)]
NEAR = [(i, i ^ 1) for i in range(32)]


def own_front(value, my_core):
    kept = lax.dynamic_index_in_dim(value, my_core, 0, keepdims=False)
    given = lax.dynamic_index_in_dim(value, 1 - my_core, 0, keepdims=False)
    return across(jnp.stack([kept, lax.ppermute(given, "col", CORE)]), FAR, "col")


def device(x, z, y, core):
    return (x * 8 + z * 2 + y % 2) * 4 + (y // 2) * 2 + core


def corner_columns(piece, moved, my_x, my_z, my_y, my_core):
    both = ("row", "col")
    got = []
    for k in range(4):
        pairs = [
            (device(2 * f, z, h, 0), device(2 * f, z, (h + k) % 4, f))
            for f in range(2) for z in range(4) for h in range(2)
        ]
        got.append(lax.ppermute(piece, both, pairs))
    got, moved = lax.optimization_barrier((got, moved))
    got = jnp.stack(got)
    pair = jnp.stack(
        [lax.dynamic_index_in_dim(got, (my_y + 4 - h) % 4, 0, keepdims=False) for h in range(2)]
    )
    away = (my_x + 4 - 2 * my_core) % 4

    def spread_x(value):
        half = value.shape[-2] // 2

        def moved(part, start, by):
            pairs = [
                (device((2 * core + start) % 4, z, y, core), device((2 * core + start + by) % 4, z, y, core))
                for z in range(4) for y in range(4) for core in range(2)
            ]
            return lax.ppermute(part, both, pairs)

        below, above = moved(value, 0, 1), moved(value, 0, -1)
        if value.ndim == 3:
            far = moved(value, 0, 2)
        else:
            far = jnp.concatenate(
                [moved(below[..., :half, :], 1, 1), moved(above[..., half:, :], 3, -1)], axis=-2
            )
        return jnp.where(away == 0, value, jnp.where(away == 1, below, jnp.where(away == 3, above, far)))

    def ring_z(value, xs):
        def moved(part, by):
            pairs = [
                (device(x, z, y, core), device(x, (z + by) % 4, y, core))
                for z in range(4) for y in range(4) for core in range(2) for x in xs(core)
            ]
            return lax.ppermute(part, both, pairs)

        return jnp.stack([value] + [moved(value, by) for by in (1, 2, -1)])

    lo = ring_z(pair[:, :512], lambda core: [2 * core])
    hi = spread_x(pair[:, 512:])
    near = across(moved, NEAR, "row")
    lo, hi, near = lax.optimization_barrier((lo, hi, near))
    return spread_x(lo), ring_z(hi, lambda core: range(4)), near


def shards(contrib, target_rows, diag_shift, pattern):
    my_row = lax.axis_index("row").astype(jnp.int32)
    my_col = lax.axis_index("col").astype(jnp.int32)
    my_core = my_col % 2
    my_x, my_z, my_y = my_row // 8, (my_row // 2) % 4, (my_col // 2) * 2 + my_row % 2
    pos = jnp.stack([my_row, my_col])
    diag = diag_shift.reshape(2, 2, 128)
    panel, marks, slots = build_head(pos, target_rows, contrib, diag)
    heads = jnp.swapaxes(marks[:4].reshape(4, 2, 16), 0, 1).reshape(2, 1, 64)
    heads = jnp.broadcast_to(heads, (2, 16, 64)).reshape(32, 64)
    marks = jnp.concatenate([marks, heads, heads[:, :32]], axis=1).astype(F32)
    panel = panel.reshape(32, 72, 128).at[:, 66, :].set(marks)
    panel = lax.all_to_all(panel, "row", split_axis=0, concat_axis=0, tiled=True)
    marks = panel[:, 66, :96].astype(jnp.int32)
    piece = panel_piece(pos, marks, pattern, panel.reshape(32 * 72, 128))
    slots, piece = lax.optimization_barrier((slots, piece))
    main = build_main(slots, contrib)
    moves = [
        (i * 4 + c, i * 4 + ((i // 2) % 4 + c) % 4) for i in range(32) for c in range(4)
    ]
    moved = lax.ppermute(piece, ("row", "col"), moves)
    corner_lo, corner_hi, pair = corner_columns(piece, moved, my_x, my_z, my_y, my_core)
    opposite = lax.ppermute(pair[:, :512], "row", turn("z", 2))
    corner_lo, corner_hi, main, pair, opposite = lax.optimization_barrier(
        (corner_lo, corner_hi, main, pair, opposite)
    )
    lo, hi = short_ring(pair[:, :512], "z", opposite), short_ring(pair[:, 512:], "x")
    main = lax.all_to_all(
        main.reshape(128, 128, 128), ("row", "col"), split_axis=0, concat_axis=0, tiled=True
    )
    lower, inverse = factor(pos, corner_lo, corner_hi)
    main, lower, lo, hi = lax.optimization_barrier((main, lower, lo, hi))
    lo, hi = ring(lo, "x"), ring(hi, "z")
    front, own_left = assemble(pos, marks, pattern, diag, main.reshape(16384, 128))
    lefts = own_front(own_left, my_core)
    w = left(pos, lefts, inverse, lower)
    kept = w[:, :1280]
    given = jnp.concatenate([w[:, :1024], w[:, 1280:]], axis=1)
    w = jnp.stack([kept, lax.ppermute(given, "col", CORE)])
    result = schur(pos, front, w, lo, hi)
    return result.reshape(2, 1, 1, 256, 8, 1, 256)


def solution(mesh):
    in_specs = (P(None, "row", "col"), P(None, "row"), P(None, None, "row", None), P())
    out_specs = P(None, None, "row", None, None, "col", None)
    return jax.shard_map(shards, mesh=mesh, in_specs=in_specs, out_specs=out_specs, check_vma=False)
```

```python
import jax
import jax.numpy as jnp
from jax import lax
from jax.experimental import pallas as pl
from jax.experimental.pallas import tpu as pltpu
from jax.sharding import PartitionSpec as P

F = 8192
P_SIZE = 1024
BS = 256
HI = lax.Precision.HIGHEST
LOW = 384
VM = pl.BlockSpec(memory_space=pltpu.VMEM)
SM = pl.BlockSpec(memory_space=pltpu.SMEM)
F32 = jnp.float32


def params():
    return pltpu.CompilerParams(vmem_limit_bytes=60 * 1024 * 1024)


def dot_nn(a, b):
    return lax.dot_general(a, b, (((1,), (0,)), ((), ())), precision=HI, preferred_element_type=F32)


def dot_nt(a, b):
    return lax.dot_general(a, b, (((1,), (1,)), ((), ())), precision=HI, preferred_element_type=F32)


def dot_tn(a, b):
    return lax.dot_general(a, b, (((0,), (0,)), ((), ())), precision=HI, preferred_element_type=F32)


def head_kernel(pos_ref, t_ref, x_ref, diag_ref, panel_ref, marks_ref, slots_ref, cnt):
    my_col = pos_ref[1]

    def clear(i, _):
        cnt[i] = 0
        for k in range(16):
            marks_ref[i // 2, (i % 2) * 16 + k] = 256
        return 0

    lax.fori_loop(0, 64, clear, 0)
    for i in range(32):
        panel_ref[pl.ds(i * 72 + 64, 2), :] = diag_ref[i // 16]

    def place_rows(group, _):
        first = pl.multiple_of(group * 8, 8)
        for f in range(2):
            for k in range(8):
                target = t_ref[f, first + k]
                owner = lax.shift_right_logical(target, 8)
                slot = cnt[f * 32 + owner]
                cnt[f * 32 + owner] = slot + 1
                marks_ref[owner, f * 16 + slot] = jnp.bitwise_and(target, 255)
                slots_ref[f, first + k] = owner * 128 + slot

                @pl.when(owner < 4)
                def _():
                    for j in range(16):
                        u, c, h = j // 8, (j // 2) % 4, j % 2
                        q = jnp.bitwise_and(c + 4 - my_col, 3)
                        dest = f * 16 + u * 8 + q * 2 + h
                        panel_ref[pl.ds(dest * 72 + owner * 16 + slot, 1), :] = (
                            x_ref[f, pl.ds(first, 8), j * 128:(j + 1) * 128][k:k + 1, :]
                        )

        return 0

    lax.fori_loop(0, 32, place_rows, 0)


def build_head(pos, targets, contrib, diag):
    return pl.pallas_call(
        head_kernel,
        out_shape=(
            jax.ShapeDtypeStruct((32 * 72, 128), F32),
            jax.ShapeDtypeStruct((32, 32), jnp.int32),
            jax.ShapeDtypeStruct((2, 256), jnp.int32),
        ),
        in_specs=[SM, SM, VM, VM],
        out_specs=(VM, SM, SM),
        scratch_shapes=[pltpu.SMEM((64,), jnp.int32)],
        compiler_params=params(),
    )(pos, targets, contrib, diag)


def main_kernel(slots_ref, x_ref, main_ref, buf):
    for f in range(2):
        for j in range(16):
            block, half = j // 2, j % 2
            place = (block % 4) * 4 + (block // 4) * 2 + half
            buf[pl.ds(f * 4096 + place, 256, stride=16), :] = x_ref[f, :, j * 128:(j + 1) * 128]

    def place_row(i, _):
        for f in range(2):
            at = slots_ref[f, i]
            source = (f * 256 + i) * 16
            for c in range(4):
                main_ref[pl.ds((at + (c * 2 + f) * 16) * 4, 4), :] = buf[pl.ds(source + c * 4, 4), :]
        return 0

    lax.fori_loop(0, 256, place_row, 0, unroll=2)


def build_main(slots, contrib):
    return pl.pallas_call(
        main_kernel,
        out_shape=jax.ShapeDtypeStruct((16384, 128), F32),
        in_specs=[SM, VM],
        out_specs=VM,
        scratch_shapes=[pltpu.VMEM((8192, 128), F32)],
        compiler_params=params(),
        cost_estimate=pl.CostEstimate(flops=10**10, bytes_accessed=2**23, transcendentals=0),
    )(slots, contrib)


def eye128():
    return (
        lax.broadcasted_iota(jnp.int32, (128, 128), 0) == lax.broadcasted_iota(jnp.int32, (128, 128), 1)
    ).astype(F32)


def panel_kernel(pos_ref, marks_ref, pattern_ref, x_ref, out_ref, acc):
    my_row, my_col = pos_ref[0], pos_ref[1]
    f, u, q, h = my_row // 16, (my_row // 8) % 2, (my_row // 2) % 4, my_row % 2
    block = 8 * my_col + u * 4 + (q + my_col) % 4
    acc[...] = jnp.zeros_like(acc)

    def source(s, _):
        def step(k, _):
            rows = [n * 264 + marks_ref[s, 32 + n * 16 + k] for n in range(4)]
            new = [
                acc[pl.ds(rows[n], 1), :] + x_ref[pl.ds(s * 72 + n * 16 + k, 1), :] for n in range(4)
            ]
            for n in range(4):
                acc[pl.ds(rows[n], 1), :] = new[n]
            return 0

        return lax.fori_loop(0, 16, step, 0, unroll=4)

    lax.fori_loop(0, 32, source, 0)
    scale = jnp.where(block >= 4, pattern_ref[f, block], 1).astype(F32)
    for n in range(4):
        out_ref[pl.ds(n * 256, 256), :] = acc[n * 264:n * 264 + 256, :] * scale

    @pl.when(block < 4)
    def _():
        start = pl.multiple_of(block * 256 + h * 128, 128)
        shift = x_ref[pl.ds(block * 72 + 64 + h, 1), :]
        out_ref[pl.ds(start, 128), :] += eye128() * shift


def panel_piece(pos, marks, pattern, received):
    return pl.pallas_call(
        panel_kernel,
        out_shape=jax.ShapeDtypeStruct((1024, 128), F32),
        in_specs=[SM, SM, SM, VM],
        out_specs=VM,
        scratch_shapes=[pltpu.VMEM((1056, 128), F32)],
        compiler_params=params(),
    )(pos, marks, pattern, received)


SRCS = 8


def assemble_kernel(pos_ref, marks_ref, pattern_ref, diag_ref, x_ref, out_ref, left_ref, acc):
    step = pl.program_id(0)
    my_row, my_col = pos_ref[0], pos_ref[1]

    @pl.when(step == 0)
    def _():
        acc[...] = jnp.zeros_like(acc)

    def source(s, _):
        def slot(k, _):
            at = [marks_ref[step * SRCS + s, f * 16 + k] * 16 for f in range(2)]
            new = [
                acc[f, pl.ds(at[f] + c * 4, 4), :]
                + x_ref[pl.ds((((s * 4 + c) * 2 + f) * 16 + k) * 4, 4), :]
                for f in range(2) for c in range(4)
            ]
            for f in range(2):
                for c in range(4):
                    acc[f, pl.ds(at[f] + c * 4, 4), :] = new[f * 4 + c]
            return 0

        return lax.fori_loop(0, 16, slot, 0)

    lax.fori_loop(0, SRCS, source, 0)

    @pl.when(step == pl.num_programs(0) - 1)
    def _():
        for f in range(2):
            scale = jnp.where(my_row >= 4, pattern_ref[f, my_row], 1).astype(F32)

            @pl.when(my_row % 4 == my_col)
            def _():
                for h in range(2):
                    at = pl.ds(h * 2048 + (my_row // 4) * 2 + h, 128, stride=16)
                    acc[f, at, :] += eye128() * diag_ref[f, h:h + 1, :]

            for h in range(2):
                left_ref[f, :, h * 128:(h + 1) * 128] = acc[f, pl.ds(h, 256, stride=16), :] * scale
            out_ref[f] = acc[f, :4096, :]


def assemble(pos, marks, pattern, diag, received):
    chunk = SRCS * 512
    return pl.pallas_call(
        assemble_kernel,
        grid=(32 // SRCS,),
        out_shape=(
            jax.ShapeDtypeStruct((2, 4096, 128), F32),
            jax.ShapeDtypeStruct((2, 256, 256), F32),
        ),
        in_specs=[SM, SM, SM, VM, pl.BlockSpec((chunk, 128), lambda s: (s, 0))],
        out_specs=(
            pl.BlockSpec((2, 4096, 128), lambda s: (0, 0, 0)),
            pl.BlockSpec((2, 256, 256), lambda s: (0, 0, 0)),
        ),
        scratch_shapes=[pltpu.VMEM((2, 4112, 128), F32)],
        compiler_params=params(),
        cost_estimate=pl.CostEstimate(flops=10**6, bytes_accessed=2**12, transcendentals=0),
    )(pos, marks, pattern, diag, received)


def factor_steps(steps, l_ref, x_ref, d_ref):
    lanes = lax.broadcasted_iota(jnp.int32, (8, 128), 1)
    subs = lax.broadcasted_iota(jnp.int32, (8, 128), 0)
    low = lax.broadcasted_iota(jnp.int32, (128, 128), 0) >= lax.broadcasted_iota(jnp.int32, (128, 128), 1)

    for p in steps:
        here = slice(p * 128, (p + 1) * 128)
        d_ref[:, :128] = l_ref[here, here]
        d_ref[:, 128:] = eye128()

        def group(g, _):
            rows = d_ref[pl.ds(pl.multiple_of(g * 8, 8), 8), :]
            a8, r8 = rows[:, :128], rows[:, 128:]
            turned = pltpu.roll(a8, (128 - g * 8) % 128, 1)
            cols = [jnp.broadcast_to(turned[:, j:j + 1], (8, 128)) for j in range(8)]
            for j in range(8):
                pivot = jnp.broadcast_to(cols[j][j:j + 1, :], (8, 128))
                root = lax.rsqrt(pivot)
                root = root * (1.5 - 0.5 * pivot * root * root)
                mult = jnp.where(subs > j, cols[j] * root, 0.0)
                for k in range(j + 1, 8):
                    cols[k] = cols[k] - mult * (cols[k][j:j + 1, :] * root)
                ua, ur = a8[j:j + 1, :] * root, r8[j:j + 1, :] * root
                a8 = jnp.where(subs == j, ua, a8 - mult * ua)
                r8 = jnp.where(subs == j, ur, r8 - mult * ur)
            new = jnp.concatenate([a8, r8], axis=1)
            d_ref[pl.ds(pl.multiple_of(g * 8, 8), 8), :] = new
            later = jnp.where(lanes > g * 8 + 7, a8, 0.0)
            d_ref[...] = d_ref[...] - dot_tn(later, new)
            return 0

        lax.fori_loop(0, 16, group, 0)
        inverse = jnp.where(low, d_ref[:, 128:], 0.0)
        l_ref[here, here] = jnp.where(low, d_ref[:, :128].T, 0.0)
        x_ref[here, here] = inverse
        if p > 0:
            done = p * 128
            both = dot_nn(l_ref[here, :done], x_ref[:done, :done])
            x_ref[here, :done] = -dot_nn(inverse, both)
        if p < 7:
            after = (p + 1) * 128
            l_ref[here, after:] = jnp.zeros((128, 1024 - after), F32)
            x_ref[here, after:] = jnp.zeros((128, 1024 - after), F32)
            l_ref[after:, here] = dot_nt(l_ref[after:, here], inverse)
            for i in range(p + 1, 8):
                mine = slice(i * 128, (i + 1) * 128)
                upto = slice(after, (i + 1) * 128)
                l_ref[mine, upto] = l_ref[mine, upto] - dot_nt(l_ref[mine, here], l_ref[upto, here])


def factor_kernel(pos_ref, lo_ref, hi_ref, l_ref, x_ref, d_ref):
    my_z = (pos_ref[0] // 2) % 4

    def corner(rows, block):
        ref, first = (lo_ref, rows * 128) if rows * 128 < LOW else (hi_ref, rows * 128 - LOW)
        return ref[jnp.bitwise_and(my_z + 4 - block // 2, 3), block % 2, first:first + 128, :]

    for i in range(8):
        for j in range(i + 1):
            l_ref[i * 128:(i + 1) * 128, j * 128:(j + 1) * 128] = 0.5 * (corner(i, j) + corner(j, i).T)
    factor_steps(range(8), l_ref, x_ref, d_ref)


def factor(pos, corner_lo, corner_hi):
    whole = jax.ShapeDtypeStruct((1024, 1024), F32)
    return pl.pallas_call(
        factor_kernel,
        out_shape=(whole, whole),
        in_specs=[SM, VM, VM],
        out_specs=(VM, VM),
        scratch_shapes=[pltpu.VMEM((128, 256), F32)],
        compiler_params=params(),
        cost_estimate=pl.CostEstimate(flops=10**11, bytes_accessed=12 * 2**20, transcendentals=0),
    )(pos, corner_lo, corner_hi)


def left_kernel(pos_ref, a_ref, x_ref, head_ref, w_ref, wide, rows):
    my_row, my_col = pos_ref[0], pos_ref[1]
    for far in range(2):
        for core in range(2):
            column = jnp.bitwise_xor(my_col, core + 2 * far)
            wide[:, pl.ds(pl.multiple_of(column * 256, 256), 256)] = a_ref[far, core]
    for b in range(4):
        here = slice(b * 256, (b + 1) * 256)
        rows[:, here] = dot_nt(wide[:, :(b + 1) * 256], x_ref[here, :(b + 1) * 256])
    for b in range(4):
        here = slice(b * 256, (b + 1) * 256)
        w_ref[:, here] = dot_nn(rows[:, b * 256:], x_ref[b * 256:, here])

    @pl.when(my_row < 4)
    def _():
        rows[...] = head_ref[...]

    for core in range(2):
        column = pl.multiple_of(jnp.bitwise_xor(my_col, core) * 256, 256)
        w_ref[:, 1024 + core * 256:1280 + core * 256] = rows[:, pl.ds(column, 256)]


def left(pos, a, inverse, lower):
    return pl.pallas_call(
        left_kernel,
        grid_spec=pltpu.PrefetchScalarGridSpec(
            num_scalar_prefetch=1,
            grid=(1,),
            in_specs=[
                pl.BlockSpec((2, 2, 256, 256), lambda i, pos: (0, 0, 0, 0)),
                pl.BlockSpec((1024, 1024), lambda i, pos: (0, 0)),
                pl.BlockSpec((256, 1024), lambda i, pos: (jnp.minimum(pos[0], 3), 0)),
            ],
            out_specs=pl.BlockSpec((256, 1536), lambda i, pos: (0, 0)),
            scratch_shapes=[pltpu.VMEM((256, 1024), F32), pltpu.VMEM((256, 1024), F32)],
        ),
        out_shape=jax.ShapeDtypeStruct((256, 1536), F32),
        compiler_params=params(),
        cost_estimate=pl.CostEstimate(flops=10**6, bytes_accessed=2**12, transcendentals=0),
    )(pos, a, inverse, lower)


def split(value):
    high = value.astype(jnp.bfloat16)
    return high, (value - high.astype(F32)).astype(jnp.bfloat16)


def dot_16(a, b):
    return lax.dot_general(a, b, (((1,), (0,)), ((), ())), preferred_element_type=F32)


def schur_kernel(table_ref, front_ref, w_ref, *refs):
    out_ref, partial, w_high, w_low = refs[10:]
    f, j = pl.program_id(0), pl.program_id(1)
    my_row = table_ref[144]
    par = jnp.bitwise_and(my_row, 1)
    block = 2 * jnp.bitwise_and(j, 3) + lax.shift_right_logical(j, 2)
    turned = (table_ref[f * 8 + j], table_ref[16 + f * 8 + j])
    places = [pl.ds(2 * block + h, 256, stride=16) for h in range(2)]

    def columns(ref, rows):
        return jnp.concatenate([ref[0, jnp.bitwise_xor(par, h), rows, :] for h in range(2)], axis=1)

    def put(value):
        for h in range(2):
            out_ref[0, places[h], :] = value[:, h * 128:(h + 1) * 128]

    @pl.when(j == 0)
    def _():
        put(w_ref[0, :, 1024:1280])
        w_high[...], w_low[...] = split(w_ref[0, :, :1024])

    for part in range(2):
        own, below, first, second, above = refs[5 * part:5 * part + 5]
        for k, sources in enumerate(((own,), (below,), (first, second), (above,))):
            here = (j > 0) & (turned[part] == k)
            rows = 512 // len(sources)

            @pl.when(here & (my_row >= 4))
            def _():
                total = 0.0
                for i, ref in enumerate(sources):
                    start = part * 512 + i * rows
                    high, low = split(columns(ref, slice(0, rows)))
                    own_high, own_low = w_high[:, start:start + rows], w_low[:, start:start + rows]
                    total += dot_16(own_high, low) + dot_16(own_low, high) + dot_16(own_high, high)
                if part == 0:
                    partial[...] = total
                else:
                    total = total + partial[...]
                    for h in range(2):
                        out_ref[0, places[h], :] = (
                            front_ref[0, places[h], :] - total[:, h * 128:(h + 1) * 128]
                        )

            for i in range(2):

                @pl.when(here & (my_row == part * 2 + i))
                def _():
                    if len(sources) == 2:
                        put(columns(sources[i], slice(0, 256)))
                    else:
                        put(columns(sources[0], slice(i * 256, (i + 1) * 256)))


def schur_steps(pos):
    step = jnp.arange(16, dtype=jnp.int32)
    x, z = step // 4, (pos[1] + 4 - step % 4) % 4
    my_x, my_z = pos[0] // 8, (pos[0] // 2) % 4
    rows = [(my_x + 4 - x) % 4, (my_z + 4 - z) % 4]
    for k in (0, 1, 2, 2, 3):
        mine = (my_x + 4 - k) % 4
        idle = jnp.where(x < mine, z[0], z[3])
        rows.append(jnp.where(x == mine, z, idle))
    rows.append(x)
    rows.append(jnp.broadcast_to(pos[1] % 2, (16,)))
    return jnp.concatenate([jnp.concatenate(rows), pos]).astype(jnp.int32)


def schur(pos, front, w, lo, hi):
    def lo_map(row):
        return lambda f, j, table: (table[row * 16 + f * 8 + j], 0, 0, 0)

    def fixed(f, j, table):
        return f, 0, 0

    rows = (512, 512, 256, 256, 512)
    return pl.pallas_call(
        schur_kernel,
        grid_spec=pltpu.PrefetchScalarGridSpec(
            num_scalar_prefetch=1,
            grid=(2, 8),
            in_specs=[
                pl.BlockSpec((1, 4096, 128), fixed),
                pl.BlockSpec(
                    (1, 256, 1280), lambda f, j, table: (jnp.bitwise_xor(f, table[128]), 0, 0)
                ),
            ]
            + [pl.BlockSpec((1, 2, n, 128), lo_map(2 + i)) for i, n in enumerate(rows)]
            + [pl.BlockSpec((1, 2, n, 128), lo_map(7)) for n in rows],
            out_specs=pl.BlockSpec((1, 4096, 128), fixed),
            scratch_shapes=[
                pltpu.VMEM((256, 256), F32),
                pltpu.VMEM((256, 1024), jnp.bfloat16),
                pltpu.VMEM((256, 1024), jnp.bfloat16),
            ],
        ),
        out_shape=jax.ShapeDtypeStruct((2, 4096, 128), F32),
        compiler_params=params(),
    )(schur_steps(pos), front, w, *lo, *hi)


def turn(axis, by):
    pairs = []
    for x in range(4):
        for z in range(4):
            for y in range(2):
                to = ((x + by) % 4, z) if axis == "x" else (x, (z + by) % 4)
                pairs.append((x * 8 + z * 2 + y, to[0] * 8 + to[1] * 2 + y))
    return pairs


def ring(value, axis):
    forth, back = turn(axis, 1), turn(axis, -1)
    half = value.shape[-2] // 2
    below = lax.ppermute(value, "row", forth)
    above = lax.ppermute(value, "row", back)
    first = lax.ppermute(below[..., :half, :], "row", forth)
    second = lax.ppermute(above[..., half:, :], "row", back)
    return value, below, first, second, above


def gathered(value, axis):
    if axis == "x":
        groups = [[x * 8 + rest for x in range(4)] for rest in range(8)]
    else:
        groups = [[x * 8 + z * 2 + y for z in range(4)] for x in range(4) for y in range(2)]
    return lax.all_gather(value, "row", axis_index_groups=groups)


def across(value, pairs, axis):
    return jnp.stack([value, lax.ppermute(value, axis, pairs)])


CORE = [(0, 1), (1, 0), (2, 3), (3, 2)]
FAR = [(0, 2), (2, 0), (1, 3), (3, 1)]
NEAR = [(i, i ^ 1) for i in range(32)]


def own_front(value, my_core):
    kept = lax.dynamic_index_in_dim(value, my_core, 0, keepdims=False)
    given = lax.dynamic_index_in_dim(value, 1 - my_core, 0, keepdims=False)
    return across(jnp.stack([kept, lax.ppermute(given, "col", CORE)]), FAR, "col")


def device(x, z, y, core):
    return (x * 8 + z * 2 + y % 2) * 4 + (y // 2) * 2 + core


def corner_columns(piece, moved, my_x, my_z, my_y, my_core):
    both = ("row", "col")
    got = []
    for k in range(4):
        pairs = [
            (device(2 * f, z, h, 0), device(2 * f, z, (h + k) % 4, f))
            for f in range(2) for z in range(4) for h in range(2)
        ]
        got.append(lax.ppermute(piece, both, pairs))
    got, moved = lax.optimization_barrier((got, moved))
    got = jnp.stack(got)
    pair = jnp.stack(
        [lax.dynamic_index_in_dim(got, (my_y + 4 - h) % 4, 0, keepdims=False) for h in range(2)]
    )
    away = (my_x + 4 - 2 * my_core) % 4

    def spread_x(value):
        half = value.shape[-2] // 2

        def moved(part, start, by):
            pairs = [
                (device((2 * core + start) % 4, z, y, core), device((2 * core + start + by) % 4, z, y, core))
                for z in range(4) for y in range(4) for core in range(2)
            ]
            return lax.ppermute(part, both, pairs)

        below, above = moved(value, 0, 1), moved(value, 0, -1)
        if value.ndim == 3:
            far = moved(value, 0, 2)
        else:
            far = jnp.concatenate(
                [moved(below[..., :half, :], 1, 1), moved(above[..., half:, :], 3, -1)], axis=-2
            )
        return jnp.where(away == 0, value, jnp.where(away == 1, below, jnp.where(away == 3, above, far)))

    def ring_z(value, xs):
        def moved(part, by):
            pairs = [
                (device(x, z, y, core), device(x, (z + by) % 4, y, core))
                for z in range(4) for y in range(4) for core in range(2) for x in xs(core)
            ]
            return lax.ppermute(part, both, pairs)

        return jnp.stack([value] + [moved(value, by) for by in (1, 2, -1)])

    lo = ring_z(pair[:, :LOW], lambda core: [2 * core])
    hi = spread_x(pair[:, LOW:])
    near = across(moved, NEAR, "row")
    lo, hi, near = lax.optimization_barrier((lo, hi, near))
    return spread_x(lo), ring_z(hi, lambda core: range(4)), near


def shards(contrib, target_rows, diag_shift, pattern):
    my_row = lax.axis_index("row").astype(jnp.int32)
    my_col = lax.axis_index("col").astype(jnp.int32)
    my_core = my_col % 2
    my_x, my_z, my_y = my_row // 8, (my_row // 2) % 4, (my_col // 2) * 2 + my_row % 2
    pos = jnp.stack([my_row, my_col])
    diag = diag_shift.reshape(2, 2, 128)
    panel, marks, slots = build_head(pos, target_rows, contrib, diag)
    heads = jnp.swapaxes(marks[:4].reshape(4, 2, 16), 0, 1).reshape(2, 1, 64)
    heads = jnp.broadcast_to(heads, (2, 16, 64)).reshape(32, 64)
    marks = jnp.concatenate([marks, heads, heads[:, :32]], axis=1).astype(F32)
    panel = panel.reshape(32, 72, 128).at[:, 66, :].set(marks)
    panel = lax.all_to_all(panel, "row", split_axis=0, concat_axis=0, tiled=True)
    marks = panel[:, 66, :96].astype(jnp.int32)
    piece = panel_piece(pos, marks, pattern, panel.reshape(32 * 72, 128))
    slots, piece = lax.optimization_barrier((slots, piece))
    main = build_main(slots, contrib)
    moves = [
        (i * 4 + c, i * 4 + ((i // 2) % 4 + c) % 4) for i in range(32) for c in range(4)
    ]
    moved = lax.ppermute(piece, ("row", "col"), moves)
    corner_lo, corner_hi, pair = corner_columns(piece, moved, my_x, my_z, my_y, my_core)
    corner_lo, corner_hi, main, pair = lax.optimization_barrier((corner_lo, corner_hi, main, pair))
    lo, hi = gathered(pair[:, :512], "z"), gathered(pair[:, 512:], "x")
    main = lax.all_to_all(
        main.reshape(128, 128, 128), ("row", "col"), split_axis=0, concat_axis=0, tiled=True
    )
    lower, inverse = factor(pos, corner_lo, corner_hi)
    main, lower, lo, hi = lax.optimization_barrier((main, lower, lo, hi))
    lo, hi = ring(lo, "x"), ring(hi, "z")
    front, own_left = assemble(pos, marks, pattern, diag, main.reshape(16384, 128))
    lefts = own_front(own_left, my_core)
    w = left(pos, lefts, inverse, lower)
    kept = w[:, :1280]
    given = jnp.concatenate([w[:, :1024], w[:, 1280:]], axis=1)
    w = jnp.stack([kept, lax.ppermute(given, "col", CORE)])
    result = schur(pos, front, w, lo, hi)
    return result.reshape(2, 1, 1, 256, 8, 1, 256)


def solution(mesh):
    in_specs = (P(None, "row", "col"), P(None, "row"), P(None, None, "row", None), P())
    out_specs = P(None, None, "row", None, None, "col", None)
    return jax.shard_map(shards, mesh=mesh, in_specs=in_specs, out_specs=out_specs, check_vma=False)
```

```python
import jax
import jax.numpy as jnp
import numpy as np
from jax import lax
from jax.experimental import pallas as pl
from jax.experimental.pallas import tpu as pltpu
from jax.sharding import PartitionSpec as P

F = 8192
P_SIZE = 1024
BS = 256
HI = lax.Precision.HIGHEST
LOW = 384
VM = pl.BlockSpec(memory_space=pltpu.VMEM)
SM = pl.BlockSpec(memory_space=pltpu.SMEM)
F32 = jnp.float32


def params():
    return pltpu.CompilerParams(vmem_limit_bytes=60 * 1024 * 1024)


def dot_nn(a, b):
    return lax.dot_general(a, b, (((1,), (0,)), ((), ())), precision=HI, preferred_element_type=F32)


def dot_nt(a, b):
    return lax.dot_general(a, b, (((1,), (1,)), ((), ())), precision=HI, preferred_element_type=F32)


def dot_tn(a, b):
    return lax.dot_general(a, b, (((0,), (0,)), ((), ())), precision=HI, preferred_element_type=F32)


def head_kernel(pos_ref, t_ref, x_ref, diag_ref, panel_ref, marks_ref, slots_ref, cnt):
    my_col = pos_ref[1]

    def clear(i, _):
        cnt[i] = 0
        for k in range(16):
            marks_ref[i // 2, (i % 2) * 16 + k] = 256
        return 0

    lax.fori_loop(0, 64, clear, 0)
    for i in range(32):
        panel_ref[pl.ds(i * 72 + 64, 2), :] = diag_ref[i // 16]

    def place_rows(group, _):
        first = pl.multiple_of(group * 8, 8)
        for f in range(2):
            for k in range(8):
                target = t_ref[f, first + k]
                owner = lax.shift_right_logical(target, 8)
                slot = cnt[f * 32 + owner]
                cnt[f * 32 + owner] = slot + 1
                marks_ref[owner, f * 16 + slot] = jnp.bitwise_and(target, 255)
                slots_ref[f, first + k] = owner * 128 + slot

                @pl.when(owner < 4)
                def _():
                    for j in range(16):
                        u, c, h = j // 8, (j // 2) % 4, j % 2
                        q = jnp.bitwise_and(c + 4 - my_col, 3)
                        dest = f * 16 + u * 8 + q * 2 + h
                        panel_ref[pl.ds(dest * 72 + owner * 16 + slot, 1), :] = (
                            x_ref[f, pl.ds(first, 8), j * 128:(j + 1) * 128][k:k + 1, :]
                        )

        return 0

    lax.fori_loop(0, 32, place_rows, 0)


def build_head(pos, targets, contrib, diag):
    return pl.pallas_call(
        head_kernel,
        out_shape=(
            jax.ShapeDtypeStruct((32 * 72, 128), F32),
            jax.ShapeDtypeStruct((32, 32), jnp.int32),
            jax.ShapeDtypeStruct((2, 256), jnp.int32),
        ),
        in_specs=[SM, SM, VM, VM],
        out_specs=(VM, SM, SM),
        scratch_shapes=[pltpu.SMEM((64,), jnp.int32)],
        compiler_params=params(),
    )(pos, targets, contrib, diag)


def main_kernel(slots_ref, x_ref, main_ref, buf):
    for f in range(2):
        for j in range(16):
            block, half = j // 2, j % 2
            place = (block % 4) * 4 + (block // 4) * 2 + half
            buf[pl.ds(f * 4096 + place, 256, stride=16), :] = x_ref[f, :, j * 128:(j + 1) * 128]

    def place_row(i, _):
        for f in range(2):
            at = slots_ref[f, i]
            source = (f * 256 + i) * 16
            for c in range(4):
                main_ref[pl.ds((at + (c * 2 + f) * 16) * 4, 4), :] = buf[pl.ds(source + c * 4, 4), :]
        return 0

    lax.fori_loop(0, 256, place_row, 0, unroll=2)


def build_main(slots, contrib):
    return pl.pallas_call(
        main_kernel,
        out_shape=jax.ShapeDtypeStruct((16384, 128), F32),
        in_specs=[SM, VM],
        out_specs=VM,
        scratch_shapes=[pltpu.VMEM((8192, 128), F32)],
        compiler_params=params(),
        cost_estimate=pl.CostEstimate(flops=10**10, bytes_accessed=2**23, transcendentals=0),
    )(slots, contrib)


def eye128():
    return (
        lax.broadcasted_iota(jnp.int32, (128, 128), 0) == lax.broadcasted_iota(jnp.int32, (128, 128), 1)
    ).astype(F32)


def panel_kernel(pos_ref, marks_ref, pattern_ref, x_ref, out_ref, acc):
    my_row, my_col = pos_ref[0], pos_ref[1]
    f, u, q, h = my_row // 16, (my_row // 8) % 2, (my_row // 2) % 4, my_row % 2
    block = 8 * my_col + u * 4 + (q + my_col) % 4
    acc[...] = jnp.zeros_like(acc)

    def source(s, _):
        def step(k, _):
            rows = [n * 264 + marks_ref[s, 32 + n * 16 + k] for n in range(4)]
            new = [
                acc[pl.ds(rows[n], 1), :] + x_ref[pl.ds(s * 72 + n * 16 + k, 1), :] for n in range(4)
            ]
            for n in range(4):
                acc[pl.ds(rows[n], 1), :] = new[n]
            return 0

        return lax.fori_loop(0, 16, step, 0, unroll=4)

    lax.fori_loop(0, 32, source, 0)
    scale = jnp.where(block >= 4, pattern_ref[f, block], 1).astype(F32)
    for n in range(4):
        out_ref[pl.ds(n * 256, 256), :] = acc[n * 264:n * 264 + 256, :] * scale

    @pl.when(block < 4)
    def _():
        start = pl.multiple_of(block * 256 + h * 128, 128)
        shift = x_ref[pl.ds(block * 72 + 64 + h, 1), :]
        out_ref[pl.ds(start, 128), :] += eye128() * shift


def panel_piece(pos, marks, pattern, received):
    return pl.pallas_call(
        panel_kernel,
        out_shape=jax.ShapeDtypeStruct((1024, 128), F32),
        in_specs=[SM, SM, SM, VM],
        out_specs=VM,
        scratch_shapes=[pltpu.VMEM((1056, 128), F32)],
        compiler_params=params(),
    )(pos, marks, pattern, received)


SRCS = 8


def assemble_kernel(pos_ref, marks_ref, pattern_ref, diag_ref, x_ref, out_ref, left_ref, acc):
    step = pl.program_id(0)
    my_row, my_col = pos_ref[0], pos_ref[1]

    @pl.when(step == 0)
    def _():
        acc[...] = jnp.zeros_like(acc)

    def source(s, _):
        def slot(k, _):
            at = [marks_ref[step * SRCS + s, f * 16 + k] * 16 for f in range(2)]
            new = [
                acc[f, pl.ds(at[f] + c * 4, 4), :]
                + x_ref[pl.ds((((s * 4 + c) * 2 + f) * 16 + k) * 4, 4), :]
                for f in range(2) for c in range(4)
            ]
            for f in range(2):
                for c in range(4):
                    acc[f, pl.ds(at[f] + c * 4, 4), :] = new[f * 4 + c]
            return 0

        return lax.fori_loop(0, 16, slot, 0)

    lax.fori_loop(0, SRCS, source, 0)

    @pl.when(step == pl.num_programs(0) - 1)
    def _():
        for f in range(2):
            scale = jnp.where(my_row >= 4, pattern_ref[f, my_row], 1).astype(F32)

            @pl.when(my_row % 4 == my_col)
            def _():
                for h in range(2):
                    at = pl.ds(h * 2048 + (my_row // 4) * 2 + h, 128, stride=16)
                    acc[f, at, :] += eye128() * diag_ref[f, h:h + 1, :]

            for h in range(2):
                left_ref[f, :, h * 128:(h + 1) * 128] = acc[f, pl.ds(h, 256, stride=16), :] * scale
            out_ref[f] = acc[f, :4096, :]


def assemble(pos, marks, pattern, diag, received):
    chunk = SRCS * 512
    return pl.pallas_call(
        assemble_kernel,
        grid=(32 // SRCS,),
        out_shape=(
            jax.ShapeDtypeStruct((2, 4096, 128), F32),
            jax.ShapeDtypeStruct((2, 256, 256), F32),
        ),
        in_specs=[SM, SM, SM, VM, pl.BlockSpec((chunk, 128), lambda s: (s, 0))],
        out_specs=(
            pl.BlockSpec((2, 4096, 128), lambda s: (0, 0, 0)),
            pl.BlockSpec((2, 256, 256), lambda s: (0, 0, 0)),
        ),
        scratch_shapes=[pltpu.VMEM((2, 4112, 128), F32)],
        compiler_params=params(),
        cost_estimate=pl.CostEstimate(flops=10**6, bytes_accessed=2**12, transcendentals=0),
    )(pos, marks, pattern, diag, received)


def factor_steps(steps, l_ref, x_ref, d_ref):
    lanes = lax.broadcasted_iota(jnp.int32, (8, 128), 1)
    subs = lax.broadcasted_iota(jnp.int32, (8, 128), 0)
    low = lax.broadcasted_iota(jnp.int32, (128, 128), 0) >= lax.broadcasted_iota(jnp.int32, (128, 128), 1)

    for p in steps:
        here = slice(p * 128, (p + 1) * 128)
        d_ref[:, :128] = l_ref[here, here]
        d_ref[:, 128:] = eye128()

        def group(g, _):
            rows = d_ref[pl.ds(pl.multiple_of(g * 8, 8), 8), :]
            a8, r8 = rows[:, :128], rows[:, 128:]
            turned = pltpu.roll(a8, (128 - g * 8) % 128, 1)
            cols = [jnp.broadcast_to(turned[:, j:j + 1], (8, 128)) for j in range(8)]
            for j in range(8):
                pivot = jnp.broadcast_to(cols[j][j:j + 1, :], (8, 128))
                root = lax.rsqrt(pivot)
                root = root * (1.5 - 0.5 * pivot * root * root)
                mult = jnp.where(subs > j, cols[j] * root, 0.0)
                for k in range(j + 1, 8):
                    cols[k] = cols[k] - mult * (cols[k][j:j + 1, :] * root)
                ua, ur = a8[j:j + 1, :] * root, r8[j:j + 1, :] * root
                a8 = jnp.where(subs == j, ua, a8 - mult * ua)
                r8 = jnp.where(subs == j, ur, r8 - mult * ur)
            new = jnp.concatenate([a8, r8], axis=1)
            d_ref[pl.ds(pl.multiple_of(g * 8, 8), 8), :] = new
            later = jnp.where(lanes > g * 8 + 7, a8, 0.0)
            d_ref[...] = d_ref[...] - dot_tn(later, new)
            return 0

        lax.fori_loop(0, 16, group, 0)
        inverse = jnp.where(low, d_ref[:, 128:], 0.0)
        l_ref[here, here] = jnp.where(low, d_ref[:, :128].T, 0.0)
        x_ref[here, here] = inverse
        if p > 0:
            done = p * 128
            both = dot_nn(l_ref[here, :done], x_ref[:done, :done])
            x_ref[here, :done] = -dot_nn(inverse, both)
        if p < 7:
            after = (p + 1) * 128
            l_ref[here, after:] = jnp.zeros((128, 1024 - after), F32)
            x_ref[here, after:] = jnp.zeros((128, 1024 - after), F32)
            l_ref[after:, here] = dot_nt(l_ref[after:, here], inverse)
            for i in range(p + 1, 8):
                mine = slice(i * 128, (i + 1) * 128)
                upto = slice(after, (i + 1) * 128)
                l_ref[mine, upto] = l_ref[mine, upto] - dot_nt(l_ref[mine, here], l_ref[upto, here])


def factor_kernel(pos_ref, lo_ref, hi_ref, l_ref, x_ref, d_ref):
    my_z = (pos_ref[0] // 2) % 4

    def corner(rows, block):
        ref, first = (lo_ref, rows * 128) if rows * 128 < LOW else (hi_ref, rows * 128 - LOW)
        return ref[jnp.bitwise_and(my_z + 4 - block // 2, 3), block % 2, first:first + 128, :]

    for i in range(8):
        for j in range(i + 1):
            l_ref[i * 128:(i + 1) * 128, j * 128:(j + 1) * 128] = 0.5 * (corner(i, j) + corner(j, i).T)
    factor_steps(range(8), l_ref, x_ref, d_ref)


def factor(pos, corner_lo, corner_hi):
    whole = jax.ShapeDtypeStruct((1024, 1024), F32)
    return pl.pallas_call(
        factor_kernel,
        out_shape=(whole, whole),
        in_specs=[SM, VM, VM],
        out_specs=(VM, VM),
        scratch_shapes=[pltpu.VMEM((128, 256), F32)],
        compiler_params=params(),
        cost_estimate=pl.CostEstimate(flops=10**11, bytes_accessed=12 * 2**20, transcendentals=0),
    )(pos, corner_lo, corner_hi)


def left_kernel(pos_ref, a_ref, x_ref, head_ref, kept_ref, given_ref, wide, rows):
    my_row, my_col = pos_ref[0], pos_ref[1]
    for far in range(2):
        for core in range(2):
            column = jnp.bitwise_xor(my_col, core + 2 * far)
            wide[:, pl.ds(pl.multiple_of(column * 256, 256), 256)] = a_ref[far, core]
    for b in range(4):
        here = slice(b * 256, (b + 1) * 256)
        rows[:, here] = dot_nt(wide[:, :(b + 1) * 256], x_ref[here, :(b + 1) * 256])
    for b in range(4):
        here = slice(b * 256, (b + 1) * 256)
        product = dot_nn(rows[:, b * 256:], x_ref[b * 256:, here])
        kept_ref[:, here] = product
        given_ref[:, here] = product

    @pl.when(my_row < 4)
    def _():
        rows[...] = head_ref[...]

    for core, ref in enumerate((kept_ref, given_ref)):
        column = pl.multiple_of(jnp.bitwise_xor(my_col, core) * 256, 256)
        ref[:, 1024:] = rows[:, pl.ds(column, 256)]


def left(pos, a, inverse, lower):
    return pl.pallas_call(
        left_kernel,
        grid_spec=pltpu.PrefetchScalarGridSpec(
            num_scalar_prefetch=1,
            grid=(1,),
            in_specs=[
                pl.BlockSpec((2, 2, 256, 256), lambda i, pos: (0, 0, 0, 0)),
                pl.BlockSpec((1024, 1024), lambda i, pos: (0, 0)),
                pl.BlockSpec((256, 1024), lambda i, pos: (jnp.minimum(pos[0], 3), 0)),
            ],
            out_specs=(pl.BlockSpec((256, 1280), lambda i, pos: (0, 0)),) * 2,
            scratch_shapes=[pltpu.VMEM((256, 1024), F32), pltpu.VMEM((256, 1024), F32)],
        ),
        out_shape=(jax.ShapeDtypeStruct((256, 1280), F32),) * 2,
        compiler_params=params(),
        cost_estimate=pl.CostEstimate(flops=10**6, bytes_accessed=2**12, transcendentals=0),
    )(pos, a, inverse, lower)


def split(value):
    high = value.astype(jnp.bfloat16)
    return high, (value - high.astype(F32)).astype(jnp.bfloat16)


def dot_16(a, b):
    return lax.dot_general(a, b, (((1,), (0,)), ((), ())), preferred_element_type=F32)


def schur_kernel(table_ref, front_ref, kept_ref, got_ref, *refs):
    out_ref, partial, w_high, w_low = refs[10:]
    f, j = pl.program_id(0), pl.program_id(1)
    my_row = table_ref[144]
    par = jnp.bitwise_and(my_row, 1)
    block = 2 * jnp.bitwise_and(j, 3) + lax.shift_right_logical(j, 2)
    turned = (table_ref[f * 8 + j], table_ref[16 + f * 8 + j])
    places = [pl.ds(2 * block + h, 256, stride=16) for h in range(2)]

    def columns(ref, rows):
        return jnp.concatenate([ref[0, jnp.bitwise_xor(par, h), rows, :] for h in range(2)], axis=1)

    def put(value):
        for h in range(2):
            out_ref[0, places[h], :] = value[:, h * 128:(h + 1) * 128]

    for other, ref in enumerate((kept_ref, got_ref)):

        @pl.when((j == 0) & (jnp.bitwise_xor(f, table_ref[128]) == other))
        def _():
            put(ref[:, 1024:])
            w_high[...], w_low[...] = split(ref[:, :1024])

    for part in range(2):
        own, below, first, second, above = refs[5 * part:5 * part + 5]
        for k, sources in enumerate(((own,), (below,), (first, second), (above,))):
            here = (j > 0) & (turned[part] == k)
            rows = 512 // len(sources)

            @pl.when(here & (my_row >= 4))
            def _():
                total = 0.0
                for i, ref in enumerate(sources):
                    start = part * 512 + i * rows
                    high, low = split(columns(ref, slice(0, rows)))
                    own_high, own_low = w_high[:, start:start + rows], w_low[:, start:start + rows]
                    total += dot_16(own_high, low) + dot_16(own_low, high) + dot_16(own_high, high)
                if part == 0:
                    partial[...] = total
                else:
                    total = total + partial[...]
                    for h in range(2):
                        out_ref[0, places[h], :] = (
                            front_ref[0, places[h], :] - total[:, h * 128:(h + 1) * 128]
                        )

            for i in range(2):

                @pl.when(here & (my_row == part * 2 + i))
                def _():
                    if len(sources) == 2:
                        put(columns(sources[i], slice(0, 256)))
                    else:
                        put(columns(sources[0], slice(i * 256, (i + 1) * 256)))


def schur_steps(pos):
    line, step = np.repeat(np.arange(10), 16).astype(np.int32), np.tile(np.arange(16), 10).astype(np.int32)
    turns = np.repeat(np.array([0, 0, 0, 1, 2, 2, 3, 0, 0, 0], np.int32), 16)
    x = step // 4
    my_row, my_col = pos[0], pos[1]
    my_x, my_z = my_row // 8, jnp.bitwise_and(my_row // 2, 3)
    z = jnp.bitwise_and(my_col + 4 - step % 4, 3)
    mine = jnp.bitwise_and(my_x + 4 - turns, 3)
    idle = jnp.where(x < mine, my_col, jnp.bitwise_and(my_col + 1, 3))
    value = jnp.where(step == 0, my_row, my_col)
    value = jnp.where(line == 8, jnp.bitwise_and(my_col, 1), value)
    value = jnp.where(line == 7, x, value)
    value = jnp.where(line < 7, jnp.where(x == mine, z, idle), value)
    value = jnp.where(line == 1, jnp.bitwise_and(my_z + 4 - z, 3), value)
    return jnp.where(line == 0, jnp.bitwise_and(my_x + 4 - x, 3), value).astype(jnp.int32)


def schur(table, front, kept, got, lo, hi):
    def lo_map(row):
        return lambda f, j, table: (table[row * 16 + f * 8 + j], 0, 0, 0)

    def fixed(f, j, table):
        return f, 0, 0

    rows = (512, 512, 256, 256, 512)
    return pl.pallas_call(
        schur_kernel,
        grid_spec=pltpu.PrefetchScalarGridSpec(
            num_scalar_prefetch=1,
            grid=(2, 8),
            in_specs=[
                pl.BlockSpec((1, 4096, 128), fixed),
                pl.BlockSpec((256, 1280), lambda f, j, table: (0, 0)),
                pl.BlockSpec((256, 1280), lambda f, j, table: (0, 0)),
            ]
            + [pl.BlockSpec((1, 2, n, 128), lo_map(2 + i)) for i, n in enumerate(rows)]
            + [pl.BlockSpec((1, 2, n, 128), lo_map(7)) for n in rows],
            out_specs=pl.BlockSpec((1, 4096, 128), fixed),
            scratch_shapes=[
                pltpu.VMEM((256, 256), F32),
                pltpu.VMEM((256, 1024), jnp.bfloat16),
                pltpu.VMEM((256, 1024), jnp.bfloat16),
            ],
        ),
        out_shape=jax.ShapeDtypeStruct((2, 4096, 128), F32),
        compiler_params=params(),
    )(table, front, kept, got, *lo, *hi)


def turn(axis, by):
    pairs = []
    for x in range(4):
        for z in range(4):
            for y in range(2):
                to = ((x + by) % 4, z) if axis == "x" else (x, (z + by) % 4)
                pairs.append((x * 8 + z * 2 + y, to[0] * 8 + to[1] * 2 + y))
    return pairs


def ring_near(value, axis):
    return lax.ppermute(value, "row", turn(axis, 1)), lax.ppermute(value, "row", turn(axis, -1))


def ring(value, below, above, axis):
    half = value.shape[-2] // 2
    first = lax.ppermute(below[..., :half, :], "row", turn(axis, 1))
    second = lax.ppermute(above[..., half:, :], "row", turn(axis, -1))
    return value, below, first, second, above


def gathered(value, axis):
    if axis == "x":
        groups = [[x * 8 + rest for x in range(4)] for rest in range(8)]
    else:
        groups = [[x * 8 + z * 2 + y for z in range(4)] for x in range(4) for y in range(2)]
    return lax.all_gather(value, "row", axis_index_groups=groups)


def across(value, pairs, axis):
    return jnp.stack([value, lax.ppermute(value, axis, pairs)])


CORE = [(0, 1), (1, 0), (2, 3), (3, 2)]
FAR = [(0, 2), (2, 0), (1, 3), (3, 1)]


def own_front(value, my_core):
    kept = lax.dynamic_index_in_dim(value, my_core, 0, keepdims=False)
    given = lax.dynamic_index_in_dim(value, 1 - my_core, 0, keepdims=False)
    return across(jnp.stack([kept, lax.ppermute(given, "col", CORE)]), FAR, "col")


def device(x, z, y, core):
    return (x * 8 + z * 2 + y % 2) * 4 + (y // 2) * 2 + core


def corner_columns(piece, moved, near, my_x, my_z, my_y, my_core):
    both = ("row", "col")
    got = []
    for k in range(4):
        pairs = [
            (device(2 * f, z, h, 0), device(2 * f, z, (h + k) % 4, f))
            for f in range(2) for z in range(4) for h in range(2)
        ]
        got.append(lax.ppermute(piece, both, pairs))
    got, moved, near = lax.optimization_barrier((got, moved, near))
    got = jnp.stack(got)
    pair = jnp.stack(
        [lax.dynamic_index_in_dim(got, (my_y + 4 - h) % 4, 0, keepdims=False) for h in range(2)]
    )
    away = (my_x + 4 - 2 * my_core) % 4

    def spread_x(value):
        half = value.shape[-2] // 2

        def moved(part, start, by):
            pairs = [
                (device((2 * core + start) % 4, z, y, core), device((2 * core + start + by) % 4, z, y, core))
                for z in range(4) for y in range(4) for core in range(2)
            ]
            return lax.ppermute(part, both, pairs)

        below, above = moved(value, 0, 1), moved(value, 0, -1)
        if value.ndim == 3:
            far = moved(value, 0, 2)
        else:
            far = jnp.concatenate(
                [moved(below[..., :half, :], 1, 1), moved(above[..., half:, :], 3, -1)], axis=-2
            )
        return jnp.where(away == 0, value, jnp.where(away == 1, below, jnp.where(away == 3, above, far)))

    def ring_z(value, xs):
        def moved(part, by):
            pairs = [
                (device(x, z, y, core), device(x, (z + by) % 4, y, core))
                for z in range(4) for y in range(4) for core in range(2) for x in xs(core)
            ]
            return lax.ppermute(part, both, pairs)

        return jnp.stack([value] + [moved(value, by) for by in (1, 2, -1)])

    lo = ring_z(pair[:, :LOW], lambda core: [2 * core])
    hi = spread_x(pair[:, LOW:])
    lo, hi = lax.optimization_barrier((lo, hi))
    return spread_x(lo), ring_z(hi, lambda core: range(4)), jnp.stack([moved, near])


def shards(contrib, target_rows, diag_shift, pattern):
    my_row = lax.axis_index("row").astype(jnp.int32)
    my_col = lax.axis_index("col").astype(jnp.int32)
    my_core = my_col % 2
    my_x, my_z, my_y = my_row // 8, (my_row // 2) % 4, (my_col // 2) * 2 + my_row % 2
    pos = jnp.stack([my_row, my_col])
    diag = diag_shift.reshape(2, 2, 128)
    panel, marks, slots = build_head(pos, target_rows, contrib, diag)
    heads = jnp.swapaxes(marks[:4].reshape(4, 2, 16), 0, 1).reshape(2, 1, 64)
    heads = jnp.broadcast_to(heads, (2, 16, 64)).reshape(32, 64)
    marks = jnp.concatenate([marks, heads, heads[:, :32]], axis=1).astype(F32)
    panel = panel.reshape(32, 72, 128).at[:, 66, :].set(marks)
    panel = lax.all_to_all(panel, "row", split_axis=0, concat_axis=0, tiled=True)
    marks = panel[:, 66, :96].astype(jnp.int32)
    piece = panel_piece(pos, marks, pattern, panel.reshape(32 * 72, 128))
    slots, piece = lax.optimization_barrier((slots, piece))
    main = build_main(slots, contrib)
    places = [(i, c, ((i // 2) % 4 + c) % 4) for i in range(32) for c in range(4)]
    moved = lax.ppermute(piece, ("row", "col"), [(i * 4 + c, i * 4 + to) for i, c, to in places])
    near = lax.ppermute(piece, ("row", "col"), [(i * 4 + c, (i ^ 1) * 4 + to) for i, c, to in places])
    corner_lo, corner_hi, pair = corner_columns(piece, moved, near, my_x, my_z, my_y, my_core)
    lo = gathered(pair[:, :512], "z")
    corner_lo, corner_hi, main, pair, table = lax.optimization_barrier(
        (corner_lo, corner_hi, main, pair, schur_steps(pos))
    )
    hi = gathered(pair[:, 512:], "x")
    main = lax.all_to_all(
        main.reshape(128, 128, 128), ("row", "col"), split_axis=0, concat_axis=0, tiled=True
    )
    lower, inverse = factor(pos, corner_lo, corner_hi)
    main, lower, lo, hi = lax.optimization_barrier((main, lower, lo, hi))
    lo_near, hi_near = ring_near(lo, "x"), ring_near(hi, "z")
    front, own_left = assemble(pos, marks, pattern, diag, main.reshape(16384, 128))
    lefts = own_front(own_left, my_core)
    lo, hi = ring(lo, *lo_near, "x"), ring(hi, *hi_near, "z")
    kept, given = left(pos, lefts, inverse, lower)
    result = schur(table, front, kept, lax.ppermute(given, "col", CORE), lo, hi)
    return result.reshape(2, 1, 1, 256, 8, 1, 256)


def solution(mesh):
    in_specs = (P(None, "row", "col"), P(None, "row"), P(None, None, "row", None), P())
    out_specs = P(None, None, "row", None, None, "col", None)
    return jax.shard_map(shards, mesh=mesh, in_specs=in_specs, out_specs=out_specs, check_vma=False)
```

```python
import jax
import jax.numpy as jnp
import numpy as np
from jax import lax
from jax.experimental import pallas as pl
from jax.experimental.pallas import tpu as pltpu
from jax.sharding import PartitionSpec as P

F = 8192
P_SIZE = 1024
BS = 256
HI = lax.Precision.HIGHEST
LOW = 384
VM = pl.BlockSpec(memory_space=pltpu.VMEM)
SM = pl.BlockSpec(memory_space=pltpu.SMEM)
F32 = jnp.float32


def params():
    return pltpu.CompilerParams(vmem_limit_bytes=60 * 1024 * 1024)


def dot_nn(a, b):
    return lax.dot_general(a, b, (((1,), (0,)), ((), ())), precision=HI, preferred_element_type=F32)


def dot_nt(a, b):
    return lax.dot_general(a, b, (((1,), (1,)), ((), ())), precision=HI, preferred_element_type=F32)


def dot_tn(a, b):
    return lax.dot_general(a, b, (((0,), (0,)), ((), ())), precision=HI, preferred_element_type=F32)


def head_kernel(pos_ref, t_ref, x_ref, diag_ref, panel_ref, marks_ref, slots_ref, cnt):
    my_col = pos_ref[1]

    def clear(i, _):
        cnt[i] = 0
        for k in range(16):
            marks_ref[i // 2, (i % 2) * 16 + k] = 256
        return 0

    lax.fori_loop(0, 64, clear, 0)
    for i in range(32):
        panel_ref[pl.ds(i * 72 + 64, 2), :] = diag_ref[i // 16]

    def place_rows(group, _):
        first = pl.multiple_of(group * 8, 8)
        for f in range(2):
            for k in range(8):
                target = t_ref[f, first + k]
                owner = lax.shift_right_logical(target, 8)
                slot = cnt[f * 32 + owner]
                cnt[f * 32 + owner] = slot + 1
                marks_ref[owner, f * 16 + slot] = jnp.bitwise_and(target, 255)
                slots_ref[f, first + k] = owner * 128 + slot

                @pl.when(owner < 4)
                def _():
                    for j in range(16):
                        u, c, h = j // 8, (j // 2) % 4, j % 2
                        q = jnp.bitwise_and(c + 4 - my_col, 3)
                        dest = f * 16 + u * 8 + q * 2 + h
                        panel_ref[pl.ds(dest * 72 + owner * 16 + slot, 1), :] = (
                            x_ref[f, pl.ds(first, 8), j * 128:(j + 1) * 128][k:k + 1, :]
                        )

        return 0

    lax.fori_loop(0, 32, place_rows, 0)


def build_head(pos, targets, contrib, diag):
    return pl.pallas_call(
        head_kernel,
        out_shape=(
            jax.ShapeDtypeStruct((32 * 72, 128), F32),
            jax.ShapeDtypeStruct((32, 32), jnp.int32),
            jax.ShapeDtypeStruct((2, 256), jnp.int32),
        ),
        in_specs=[SM, SM, VM, VM],
        out_specs=(VM, SM, SM),
        scratch_shapes=[pltpu.SMEM((64,), jnp.int32)],
        compiler_params=params(),
    )(pos, targets, contrib, diag)


def main_kernel(slots_ref, x_ref, main_ref, buf):
    for f in range(2):
        for j in range(16):
            block, half = j // 2, j % 2
            place = (block % 4) * 4 + (block // 4) * 2 + half
            buf[pl.ds(f * 4096 + place, 256, stride=16), :] = x_ref[f, :, j * 128:(j + 1) * 128]

    def place_row(i, _):
        for f in range(2):
            at = slots_ref[f, i]
            source = (f * 256 + i) * 16
            for c in range(4):
                main_ref[pl.ds((at + (c * 2 + f) * 16) * 4, 4), :] = buf[pl.ds(source + c * 4, 4), :]
        return 0

    lax.fori_loop(0, 256, place_row, 0, unroll=2)


def build_main(slots, contrib):
    return pl.pallas_call(
        main_kernel,
        out_shape=jax.ShapeDtypeStruct((16384, 128), F32),
        in_specs=[SM, VM],
        out_specs=VM,
        scratch_shapes=[pltpu.VMEM((8192, 128), F32)],
        compiler_params=params(),
        cost_estimate=pl.CostEstimate(flops=10**10, bytes_accessed=2**23, transcendentals=0),
    )(slots, contrib)


def eye128():
    return (
        lax.broadcasted_iota(jnp.int32, (128, 128), 0) == lax.broadcasted_iota(jnp.int32, (128, 128), 1)
    ).astype(F32)


def panel_kernel(pos_ref, marks_ref, pattern_ref, x_ref, out_ref, acc):
    my_row, my_col = pos_ref[0], pos_ref[1]
    f, u, q, h = my_row // 16, (my_row // 8) % 2, (my_row // 2) % 4, my_row % 2
    block = 8 * my_col + u * 4 + (q + my_col) % 4
    acc[...] = jnp.zeros_like(acc)

    def source(s, _):
        def step(k, _):
            rows = [n * 264 + marks_ref[s, 32 + n * 16 + k] for n in range(4)]
            new = [
                acc[pl.ds(rows[n], 1), :] + x_ref[pl.ds(s * 72 + n * 16 + k, 1), :] for n in range(4)
            ]
            for n in range(4):
                acc[pl.ds(rows[n], 1), :] = new[n]
            return 0

        return lax.fori_loop(0, 16, step, 0, unroll=4)

    lax.fori_loop(0, 32, source, 0)
    scale = jnp.where(block >= 4, pattern_ref[f, block], 1).astype(F32)
    for n in range(4):
        out_ref[pl.ds(n * 256, 256), :] = acc[n * 264:n * 264 + 256, :] * scale

    @pl.when(block < 4)
    def _():
        start = pl.multiple_of(block * 256 + h * 128, 128)
        shift = x_ref[pl.ds(block * 72 + 64 + h, 1), :]
        out_ref[pl.ds(start, 128), :] += eye128() * shift


def panel_piece(pos, marks, pattern, received):
    return pl.pallas_call(
        panel_kernel,
        out_shape=jax.ShapeDtypeStruct((1024, 128), F32),
        in_specs=[SM, SM, SM, VM],
        out_specs=VM,
        scratch_shapes=[pltpu.VMEM((1056, 128), F32)],
        compiler_params=params(),
    )(pos, marks, pattern, received)


SRCS = 8


def assemble_kernel(pos_ref, marks_ref, pattern_ref, diag_ref, x_ref, out_ref, left_ref, acc):
    step = pl.program_id(0)
    my_row, my_col = pos_ref[0], pos_ref[1]

    @pl.when(step == 0)
    def _():
        acc[...] = jnp.zeros_like(acc)

    def source(s, _):
        def slot(k, _):
            at = [marks_ref[step * SRCS + s, f * 16 + k] * 16 for f in range(2)]
            new = [
                acc[f, pl.ds(at[f] + c * 4, 4), :]
                + x_ref[pl.ds((((s * 4 + c) * 2 + f) * 16 + k) * 4, 4), :]
                for f in range(2) for c in range(4)
            ]
            for f in range(2):
                for c in range(4):
                    acc[f, pl.ds(at[f] + c * 4, 4), :] = new[f * 4 + c]
            return 0

        return lax.fori_loop(0, 16, slot, 0)

    lax.fori_loop(0, SRCS, source, 0)

    @pl.when(step == pl.num_programs(0) - 1)
    def _():
        for f in range(2):
            scale = jnp.where(my_row >= 4, pattern_ref[f, my_row], 1).astype(F32)

            @pl.when(my_row % 4 == my_col)
            def _():
                for h in range(2):
                    at = pl.ds(h * 2048 + (my_row // 4) * 2 + h, 128, stride=16)
                    acc[f, at, :] += eye128() * diag_ref[f, h:h + 1, :]

            for h in range(2):
                left_ref[f, :, h * 128:(h + 1) * 128] = acc[f, pl.ds(h, 256, stride=16), :] * scale
            out_ref[f] = acc[f, :4096, :]


def assemble(pos, marks, pattern, diag, received):
    chunk = SRCS * 512
    return pl.pallas_call(
        assemble_kernel,
        grid=(32 // SRCS,),
        out_shape=(
            jax.ShapeDtypeStruct((2, 4096, 128), F32),
            jax.ShapeDtypeStruct((2, 256, 256), F32),
        ),
        in_specs=[SM, SM, SM, VM, pl.BlockSpec((chunk, 128), lambda s: (s, 0))],
        out_specs=(
            pl.BlockSpec((2, 4096, 128), lambda s: (0, 0, 0)),
            pl.BlockSpec((2, 256, 256), lambda s: (0, 0, 0)),
        ),
        scratch_shapes=[pltpu.VMEM((2, 4112, 128), F32)],
        compiler_params=params(),
        cost_estimate=pl.CostEstimate(flops=10**6, bytes_accessed=2**12, transcendentals=0),
    )(pos, marks, pattern, diag, received)


def factor_steps(steps, l_ref, x_ref, d_ref):
    lanes = lax.broadcasted_iota(jnp.int32, (8, 128), 1)
    subs = lax.broadcasted_iota(jnp.int32, (8, 128), 0)
    low = lax.broadcasted_iota(jnp.int32, (128, 128), 0) >= lax.broadcasted_iota(jnp.int32, (128, 128), 1)

    for p in steps:
        here = slice(p * 128, (p + 1) * 128)
        d_ref[:, :128] = l_ref[here, here]
        d_ref[:, 128:] = eye128()

        def group(g, _):
            rows = d_ref[pl.ds(pl.multiple_of(g * 8, 8), 8), :]
            a8, r8 = rows[:, :128], rows[:, 128:]
            turned = pltpu.roll(a8, (128 - g * 8) % 128, 1)
            cols = [jnp.broadcast_to(turned[:, j:j + 1], (8, 128)) for j in range(8)]
            for j in range(8):
                pivot = jnp.broadcast_to(cols[j][j:j + 1, :], (8, 128))
                root = lax.rsqrt(pivot)
                root = root * (1.5 - 0.5 * pivot * root * root)
                mult = jnp.where(subs > j, cols[j] * root, 0.0)
                for k in range(j + 1, 8):
                    cols[k] = cols[k] - mult * (cols[k][j:j + 1, :] * root)
                ua, ur = a8[j:j + 1, :] * root, r8[j:j + 1, :] * root
                a8 = jnp.where(subs == j, ua, a8 - mult * ua)
                r8 = jnp.where(subs == j, ur, r8 - mult * ur)
            new = jnp.concatenate([a8, r8], axis=1)
            d_ref[pl.ds(pl.multiple_of(g * 8, 8), 8), :] = new
            later = jnp.where(lanes > g * 8 + 7, a8, 0.0)
            d_ref[...] = d_ref[...] - dot_tn(later, new)
            return 0

        lax.fori_loop(0, 16, group, 0)
        inverse = jnp.where(low, d_ref[:, 128:], 0.0)
        l_ref[here, here] = jnp.where(low, d_ref[:, :128].T, 0.0)
        x_ref[here, here] = inverse
        if p > 0:
            done = p * 128
            both = dot_nn(l_ref[here, :done], x_ref[:done, :done])
            x_ref[here, :done] = -dot_nn(inverse, both)
        if p < 7:
            after = (p + 1) * 128
            l_ref[here, after:] = jnp.zeros((128, 1024 - after), F32)
            x_ref[here, after:] = jnp.zeros((128, 1024 - after), F32)
            l_ref[after:, here] = dot_nt(l_ref[after:, here], inverse)
            for i in range(p + 1, 8):
                mine = slice(i * 128, (i + 1) * 128)
                upto = slice(after, (i + 1) * 128)
                l_ref[mine, upto] = l_ref[mine, upto] - dot_nt(l_ref[mine, here], l_ref[upto, here])


def factor_kernel(pos_ref, lo_ref, hi_ref, l_ref, x_ref, d_ref):
    my_z = (pos_ref[0] // 2) % 4

    def corner(rows, block):
        ref, first = (lo_ref, rows * 128) if rows * 128 < LOW else (hi_ref, rows * 128 - LOW)
        return ref[jnp.bitwise_and(my_z + 4 - block // 2, 3), block % 2, first:first + 128, :]

    for i in range(8):
        for j in range(i + 1):
            l_ref[i * 128:(i + 1) * 128, j * 128:(j + 1) * 128] = 0.5 * (corner(i, j) + corner(j, i).T)
    factor_steps(range(8), l_ref, x_ref, d_ref)


def factor(pos, corner_lo, corner_hi):
    whole = jax.ShapeDtypeStruct((1024, 1024), F32)
    return pl.pallas_call(
        factor_kernel,
        out_shape=(whole, whole),
        in_specs=[SM, VM, VM],
        out_specs=(VM, VM),
        scratch_shapes=[pltpu.VMEM((128, 256), F32)],
        compiler_params=params(),
        cost_estimate=pl.CostEstimate(flops=10**11, bytes_accessed=12 * 2**20, transcendentals=0),
    )(pos, corner_lo, corner_hi)


def left_kernel(pos_ref, a_ref, x_ref, head_ref, kept_ref, given_ref, wide, rows):
    my_row, my_col = pos_ref[0], pos_ref[1]
    for far in range(2):
        for core in range(2):
            column = jnp.bitwise_xor(my_col, core + 2 * far)
            wide[:, pl.ds(pl.multiple_of(column * 256, 256), 256)] = a_ref[far, core]
    for b in range(4):
        here = slice(b * 256, (b + 1) * 256)
        rows[:, here] = dot_nt(wide[:, :(b + 1) * 256], x_ref[here, :(b + 1) * 256])
    for b in range(4):
        here = slice(b * 256, (b + 1) * 256)
        product = dot_nn(rows[:, b * 256:], x_ref[b * 256:, here])
        kept_ref[:, here] = product
        given_ref[:, here] = product

    @pl.when(my_row < 4)
    def _():
        rows[...] = head_ref[...]

    for core, ref in enumerate((kept_ref, given_ref)):
        column = pl.multiple_of(jnp.bitwise_xor(my_col, core) * 256, 256)
        ref[:, 1024:] = rows[:, pl.ds(column, 256)]


def left(pos, a, inverse, lower):
    return pl.pallas_call(
        left_kernel,
        grid_spec=pltpu.PrefetchScalarGridSpec(
            num_scalar_prefetch=1,
            grid=(1,),
            in_specs=[
                pl.BlockSpec((2, 2, 256, 256), lambda i, pos: (0, 0, 0, 0)),
                pl.BlockSpec((1024, 1024), lambda i, pos: (0, 0)),
                pl.BlockSpec((256, 1024), lambda i, pos: (jnp.minimum(pos[0], 3), 0)),
            ],
            out_specs=(pl.BlockSpec((256, 1280), lambda i, pos: (0, 0)),) * 2,
            scratch_shapes=[pltpu.VMEM((256, 1024), F32), pltpu.VMEM((256, 1024), F32)],
        ),
        out_shape=(jax.ShapeDtypeStruct((256, 1280), F32),) * 2,
        compiler_params=params(),
        cost_estimate=pl.CostEstimate(flops=10**6, bytes_accessed=2**12, transcendentals=0),
    )(pos, a, inverse, lower)


def split(value):
    high = value.astype(jnp.bfloat16)
    return high, (value - high.astype(F32)).astype(jnp.bfloat16)


def dot_16(a, b):
    return lax.dot_general(a, b, (((1,), (0,)), ((), ())), preferred_element_type=F32)


def schur_kernel(table_ref, front_ref, kept_ref, got_ref, *refs):
    out_ref, partial, w_high, w_low = refs[10:]
    f, j = pl.program_id(0), pl.program_id(1)
    my_row = table_ref[144]
    par = jnp.bitwise_and(my_row, 1)
    block = 2 * jnp.bitwise_and(j, 3) + lax.shift_right_logical(j, 2)
    turned = (table_ref[f * 8 + j], table_ref[16 + f * 8 + j])
    places = [pl.ds(2 * block + h, 256, stride=16) for h in range(2)]

    def columns(ref, rows):
        return jnp.concatenate([ref[0, jnp.bitwise_xor(par, h), rows, :] for h in range(2)], axis=1)

    def put(value):
        for h in range(2):
            out_ref[0, places[h], :] = value[:, h * 128:(h + 1) * 128]

    for other, ref in enumerate((kept_ref, got_ref)):

        @pl.when((j == 0) & (jnp.bitwise_xor(f, table_ref[128]) == other))
        def _():
            put(ref[:, 1024:])
            w_high[...], w_low[...] = split(ref[:, :1024])

    for part in range(2):
        own, below, first, second, above = refs[5 * part:5 * part + 5]
        for k, sources in enumerate(((own,), (below,), (first, second), (above,))):
            here = (j > 0) & (turned[part] == k)
            rows = 512 // len(sources)

            @pl.when(here & (my_row >= 4))
            def _():
                total = 0.0
                for i, ref in enumerate(sources):
                    start = part * 512 + i * rows
                    high, low = split(columns(ref, slice(0, rows)))
                    own_high, own_low = w_high[:, start:start + rows], w_low[:, start:start + rows]
                    total += dot_16(own_high, low) + dot_16(own_low, high) + dot_16(own_high, high)
                if part == 0:
                    partial[...] = total
                else:
                    total = total + partial[...]
                    for h in range(2):
                        out_ref[0, places[h], :] = (
                            front_ref[0, places[h], :] - total[:, h * 128:(h + 1) * 128]
                        )

            for i in range(2):

                @pl.when(here & (my_row == part * 2 + i))
                def _():
                    if len(sources) == 2:
                        put(columns(sources[i], slice(0, 256)))
                    else:
                        put(columns(sources[0], slice(i * 256, (i + 1) * 256)))


def schur_steps(pos):
    line, step = np.repeat(np.arange(10), 16).astype(np.int32), np.tile(np.arange(16), 10).astype(np.int32)
    turns = np.repeat(np.array([0, 0, 0, 1, 2, 2, 3, 0, 0, 0], np.int32), 16)
    x = step // 4
    my_row, my_col = pos[0], pos[1]
    my_x, my_z = my_row // 8, jnp.bitwise_and(my_row // 2, 3)
    z = jnp.bitwise_and(my_col + 4 - step % 4, 3)
    mine = jnp.bitwise_and(my_x + 4 - turns, 3)
    z_turn = jnp.bitwise_and(my_z + 4 - z, 3)
    idle = jnp.bitwise_and(my_z + 4 - jnp.where(x < mine, my_col, jnp.bitwise_and(my_col + 1, 3)), 3)
    value = jnp.where(step == 0, my_row, my_col)
    value = jnp.where(line == 8, jnp.bitwise_and(my_col, 1), value)
    value = jnp.where(line == 7, jnp.bitwise_and(my_x + 4 - x, 3), value)
    value = jnp.where(line < 7, jnp.where(x == mine, z_turn, idle), value)
    value = jnp.where(line == 1, z_turn, value)
    return jnp.where(line == 0, jnp.bitwise_and(my_x + 4 - x, 3), value).astype(jnp.int32)


def schur(table, front, kept, got, lo, hi):
    def lo_map(row):
        return lambda f, j, table: (table[row * 16 + f * 8 + j], 0, 0, 0)

    def fixed(f, j, table):
        return f, 0, 0

    rows = (512, 512, 256, 256, 512)
    return pl.pallas_call(
        schur_kernel,
        grid_spec=pltpu.PrefetchScalarGridSpec(
            num_scalar_prefetch=1,
            grid=(2, 8),
            in_specs=[
                pl.BlockSpec((1, 4096, 128), fixed),
                pl.BlockSpec((256, 1280), lambda f, j, table: (0, 0)),
                pl.BlockSpec((256, 1280), lambda f, j, table: (0, 0)),
            ]
            + [pl.BlockSpec((1, 2, n, 128), lo_map(2 + i)) for i, n in enumerate(rows)]
            + [pl.BlockSpec((1, 2, n, 128), lo_map(7)) for n in rows],
            out_specs=pl.BlockSpec((1, 4096, 128), fixed),
            scratch_shapes=[
                pltpu.VMEM((256, 256), F32),
                pltpu.VMEM((256, 1024), jnp.bfloat16),
                pltpu.VMEM((256, 1024), jnp.bfloat16),
            ],
        ),
        out_shape=jax.ShapeDtypeStruct((2, 4096, 128), F32),
        compiler_params=params(),
    )(table, front, kept, got, *lo, *hi)


def turn(axis, by):
    pairs = []
    for x in range(4):
        for z in range(4):
            for y in range(2):
                to = ((x + by) % 4, z) if axis == "x" else (x, (z + by) % 4)
                pairs.append((x * 8 + z * 2 + y, to[0] * 8 + to[1] * 2 + y))
    return pairs


def ring_near(value, axis):
    return lax.ppermute(value, "row", turn(axis, 1)), lax.ppermute(value, "row", turn(axis, -1))


def ring(value, below, above, axis):
    half = value.shape[-2] // 2
    first = lax.ppermute(below[..., :half, :], "row", turn(axis, 1))
    second = lax.ppermute(above[..., half:, :], "row", turn(axis, -1))
    return value, below, first, second, above


def short_ring(value, axis, opposite):
    below, above = ring_near(value, axis)
    return jnp.stack([value, below, opposite, above])


def across(value, pairs, axis):
    return jnp.stack([value, lax.ppermute(value, axis, pairs)])


CORE = [(0, 1), (1, 0), (2, 3), (3, 2)]
FAR = [(0, 2), (2, 0), (1, 3), (3, 1)]


def own_front(value, my_core):
    kept = lax.dynamic_index_in_dim(value, my_core, 0, keepdims=False)
    given = lax.dynamic_index_in_dim(value, 1 - my_core, 0, keepdims=False)
    return across(jnp.stack([kept, lax.ppermute(given, "col", CORE)]), FAR, "col")


def device(x, z, y, core):
    return (x * 8 + z * 2 + y % 2) * 4 + (y // 2) * 2 + core


def corner_columns(piece, moved, near, my_x, my_z, my_y, my_core):
    both = ("row", "col")
    got = []
    for k in range(4):
        pairs = [
            (device(2 * f, z, h, 0), device(2 * f, z, (h + k) % 4, f))
            for f in range(2) for z in range(4) for h in range(2)
        ]
        got.append(lax.ppermute(piece, both, pairs))
    got, moved, near = lax.optimization_barrier((got, moved, near))
    got = jnp.stack(got)
    pair = jnp.stack(
        [lax.dynamic_index_in_dim(got, (my_y + 4 - h) % 4, 0, keepdims=False) for h in range(2)]
    )
    away = (my_x + 4 - 2 * my_core) % 4

    def spread_x(value):
        half = value.shape[-2] // 2

        def moved(part, start, by):
            pairs = [
                (device((2 * core + start) % 4, z, y, core), device((2 * core + start + by) % 4, z, y, core))
                for z in range(4) for y in range(4) for core in range(2)
            ]
            return lax.ppermute(part, both, pairs)

        below, above = moved(value, 0, 1), moved(value, 0, -1)
        if value.ndim == 3:
            far = moved(value, 0, 2)
        else:
            far = jnp.concatenate(
                [moved(below[..., :half, :], 1, 1), moved(above[..., half:, :], 3, -1)], axis=-2
            )
        return jnp.where(away == 0, value, jnp.where(away == 1, below, jnp.where(away == 3, above, far)))

    def ring_z(value, xs):
        def moved(part, by):
            pairs = [
                (device(x, z, y, core), device(x, (z + by) % 4, y, core))
                for z in range(4) for y in range(4) for core in range(2) for x in xs(core)
            ]
            return lax.ppermute(part, both, pairs)

        return jnp.stack([value] + [moved(value, by) for by in (1, 2, -1)])

    lo = ring_z(pair[:, :LOW], lambda core: [2 * core])
    hi = spread_x(pair[:, LOW:])
    panel = jnp.stack([moved, near])
    opposite = lax.ppermute(panel[:, :512], "row", turn("z", 2))
    lo, hi, opposite = lax.optimization_barrier((lo, hi, opposite))
    return spread_x(lo), ring_z(hi, lambda core: range(4)), panel, opposite


def shards(contrib, target_rows, diag_shift, pattern):
    my_row = lax.axis_index("row").astype(jnp.int32)
    my_col = lax.axis_index("col").astype(jnp.int32)
    my_core = my_col % 2
    my_x, my_z, my_y = my_row // 8, (my_row // 2) % 4, (my_col // 2) * 2 + my_row % 2
    pos = jnp.stack([my_row, my_col])
    diag = diag_shift.reshape(2, 2, 128)
    panel, marks, slots = build_head(pos, target_rows, contrib, diag)
    heads = jnp.swapaxes(marks[:4].reshape(4, 2, 16), 0, 1).reshape(2, 1, 64)
    heads = jnp.broadcast_to(heads, (2, 16, 64)).reshape(32, 64)
    marks = jnp.concatenate([marks, heads, heads[:, :32]], axis=1).astype(F32)
    panel = panel.reshape(32, 72, 128).at[:, 66, :].set(marks)
    panel = lax.all_to_all(panel, "row", split_axis=0, concat_axis=0, tiled=True)
    marks = panel[:, 66, :96].astype(jnp.int32)
    piece = panel_piece(pos, marks, pattern, panel.reshape(32 * 72, 128))
    slots, piece = lax.optimization_barrier((slots, piece))
    main = build_main(slots, contrib)
    places = [(i, c, ((i // 2) % 4 + c) % 4) for i in range(32) for c in range(4)]
    moved = lax.ppermute(piece, ("row", "col"), [(i * 4 + c, i * 4 + to) for i, c, to in places])
    near = lax.ppermute(piece, ("row", "col"), [(i * 4 + c, (i ^ 1) * 4 + to) for i, c, to in places])
    corner_lo, corner_hi, pair, opposite = corner_columns(
        piece, moved, near, my_x, my_z, my_y, my_core
    )
    corner_lo, corner_hi, main, pair, table = lax.optimization_barrier(
        (corner_lo, corner_hi, main, pair, schur_steps(pos))
    )
    lo = short_ring(pair[:, :512], "z", opposite)
    hi = short_ring(pair[:, 512:], "x", lax.ppermute(pair[:, 512:], "row", turn("x", 2)))
    main = lax.all_to_all(
        main.reshape(128, 128, 128), ("row", "col"), split_axis=0, concat_axis=0, tiled=True
    )
    lower, inverse = factor(pos, corner_lo, corner_hi)
    main, lower, lo, hi = lax.optimization_barrier((main, lower, lo, hi))
    lo_near, hi_near = ring_near(lo, "x"), ring_near(hi, "z")
    front, own_left = assemble(pos, marks, pattern, diag, main.reshape(16384, 128))
    lefts = own_front(own_left, my_core)
    lo, hi = ring(lo, *lo_near, "x"), ring(hi, *hi_near, "z")
    kept, given = left(pos, lefts, inverse, lower)
    result = schur(table, front, kept, lax.ppermute(given, "col", CORE), lo, hi)
    return result.reshape(2, 1, 1, 256, 8, 1, 256)


def solution(mesh):
    in_specs = (P(None, "row", "col"), P(None, "row"), P(None, None, "row", None), P())
    out_specs = P(None, None, "row", None, None, "col", None)
    return jax.shard_map(shards, mesh=mesh, in_specs=in_specs, out_specs=out_specs, check_vma=False)
```
